32 devices in a mesh: cell: 8 (over z, core), vel: 4 (over y, x).
Axes of the slice: x: 2, y: 2, z: 4, core: 2. Of those that a mesh axis runs over, the one named last changes fastest.
Arguments:
- distribution: float32 [64, 64, 4096], P(None, 'cell', 'vel'), may hold values from 0.2 to 2
- cell_type: int32 [64, 64], P(None, 'cell'), may hold values from 0 to 2, as said below
- first_kernel: float32 [16, 4096], replicated, may hold values from -1.5 to 1.5
- second_kernel: float32 [16, 4096], replicated, may hold values from -1.5 to 1.5
- loss_kernel: float32 [4096], replicated, may hold values from -4 to 4
Outputs:
- updated: float32 [64, 64, 4096], P(None, 'cell', 'vel')
The draws below stay inside these ranges and needn't reach their ends.
Inputs may be any that keep to these rules, and one draw needn't show every extreme that they name: `cell_type`: cells with x = 0, x = 63 or y = 0 are 1, the other cells with y = 63 are 2, and every other cell is 1 with probability 1/40, else 0.
All inputs are finite; a program needn't handle non-finite values.
Results may differ from the reference program's by a relative error of at most 0.0004.
Values sent between devices are 32-bit elements; how exact they have to be, the bound alone decides.
No kernel may reach another device: no remote copies, remote signals or barrier semaphores. Data moves between devices by JAX's collectives and lax.ppermute only.
A program may use at most 128 MiB of HBM per device.

```python
import math
import jax
import jax.numpy as jnp
from jax import lax

NVEL = 16
DIRS = 16
SLAB = 16
CY = 8
VEL = 4096
NX = 64
NY = 64
N_CELL = 8
N_VEL = 4


def mirror(values, axes):
    return jnp.roll(jnp.flip(values, axes), tuple((1 for axis_item in axes)), axes)


def draw_first_kernel(key, part):
    subkey = jax.random.fold_in(key, 11)
    raw = 0.3 * jax.random.normal(subkey, (DIRS, NVEL, NVEL, NVEL), jnp.float32)
    even = 0.5 * (raw + mirror(raw, (1, 2, 3)))
    return jnp.clip(even, -1.5, 1.5).reshape(DIRS, NVEL ** 3)


def draw_second_kernel(key, part):
    subkey = jax.random.fold_in(key, 12)
    raw = 0.3 * jax.random.normal(subkey, (DIRS, NVEL, NVEL, NVEL), jnp.float32)
    even = 0.5 * (raw + mirror(raw, (1, 2, 3)))
    return jnp.clip(even, -1.5, 1.5).reshape(DIRS, NVEL ** 3)


def draw_loss_kernel(key, part):
    subkey = jax.random.fold_in(key, 13)
    raw = jax.random.normal(subkey, (NVEL, NVEL, NVEL), jnp.float32)
    even = 0.5 * (raw + mirror(raw, (0, 1, 2)))
    return jnp.clip(even, -4.0, 4.0).reshape(NVEL ** 3)


def draw_cell_type(key, part):
    row_index = jnp.arange(NX, dtype=jnp.int32)[:, None]
    col_index = jnp.arange(NY, dtype=jnp.int32)[None, :]
    lottery = jax.random.randint(jax.random.fold_in(key, 14), (NX, NY), 0, 40)
    obstacle = jnp.where(lottery == 0, 1, 0)
    side_wall = (row_index == 0) | (row_index == NX - 1) | (col_index == 0)
    lid_cells = col_index == NY - 1
    return jnp.where(side_wall, 1, jnp.where(lid_cells, 2, obstacle)).astype(jnp.int32)


def steps_of(rng, shape, cuts, low, high):
    level = 1.0
    for axis_at, blocks in cuts:
        steps = jax.random.uniform(jax.random.fold_in(jax.random.fold_in(rng, 6), axis_at), (blocks,), jnp.float32, low / len(cuts), high / len(cuts))
        level = level * jnp.repeat(jnp.exp(steps), shape[axis_at] // blocks).reshape((-1,) + (1,) * (len(shape) - 1 - axis_at))
    return level


def setup_inputs(seed: int = 0) -> dict:
    splits = jax.random.split(jax.random.key(seed), 6)
    distribution = jnp.clip(jnp.exp(math.log(2.0) - 2.3025851 * jax.random.uniform(splits[0], (NX, NY, VEL), jnp.float32) ** steps_of(splits[0], (NX, NY, VEL), ((1, 8), (2, 4)), -0.2, 0.2)), 0.2, 2.0)
    cell_type = draw_cell_type(jax.random.fold_in(splits[5], 71), 0)
    first_kernel = draw_first_kernel(jax.random.fold_in(splits[5], 71), 0)
    second_kernel = draw_second_kernel(jax.random.fold_in(splits[5], 71), 0)
    loss_kernel = draw_loss_kernel(jax.random.fold_in(splits[5], 71), 0)
    return {"distribution": distribution, "cell_type": cell_type, "first_kernel": first_kernel, "second_kernel": second_kernel, "loss_kernel": loss_kernel}


courant = 0.45
collision_timestep = 0.1
pass_forms = ("ai,ijkc->ajkc", "aj,ijkc->iakc", "ak,ijkc->ijac")


def components(nvel):
    levels = (2.0 * jnp.arange(nvel, dtype=jnp.float32) - (nvel - 1)) / (nvel - 1)
    along_x = jnp.repeat(levels, nvel * nvel)
    along_y = jnp.tile(jnp.repeat(levels, nvel), nvel)
    along_z = jnp.tile(levels, nvel * nvel)
    return along_x, along_y, along_z


def wall_tables(along_x, along_y, along_z):
    still_wall = jnp.exp(-4.5 * (along_x * along_x + along_y * along_y + along_z * along_z))
    still_wall = still_wall / jnp.sum(still_wall)
    moving = jnp.exp(-0.5 * ((3.0 * along_x - 1.0) ** 2 + 9.0 * along_y * along_y + 9.0 * along_z * along_z))
    moving = moving / jnp.sum(moving)
    return still_wall, moving


def fourier_tables(nvel):
    indices = jnp.arange(nvel, dtype=jnp.int32)
    angles = 2.0 * math.pi * ((indices[:, None] * indices[None, :]) % nvel).astype(jnp.float32) / nvel
    cosine = jnp.cos(angles)
    sine_part = jnp.sin(angles)
    return (cosine.astype(jnp.bfloat16), (-sine_part).astype(jnp.bfloat16),
            (cosine / nvel).astype(jnp.bfloat16), (sine_part / nvel).astype(jnp.bfloat16))


def apply_table(matrix, operand, pattern):
    return jnp.einsum(pattern, matrix.astype(jnp.float32), operand.astype(jnp.float32), precision=lax.Precision.HIGHEST)


def real_pass(operand, cos_table, sin_table, pattern):
    return apply_table(cos_table, operand, pattern).astype(jnp.bfloat16), apply_table(sin_table, operand, pattern).astype(jnp.bfloat16)


def complex_pass(real_part, imag_part, cos_table, sin_table, pattern):
    new_real = apply_table(cos_table, real_part, pattern) - apply_table(sin_table, imag_part, pattern)
    new_imag = apply_table(cos_table, imag_part, pattern) + apply_table(sin_table, real_part, pattern)
    return new_real.astype(jnp.bfloat16), new_imag.astype(jnp.bfloat16)


def last_pass(real_part, imag_part, cos_table, sin_table, pattern):
    return apply_table(cos_table, real_part, pattern) - apply_table(sin_table, imag_part, pattern)


def spectrum_of(rounded, tables):
    real_part, imag_part = real_pass(rounded, tables[0], tables[1], pass_forms[0])
    real_part, imag_part = complex_pass(real_part, imag_part, tables[0], tables[1], pass_forms[1])
    return complex_pass(real_part, imag_part, tables[0], tables[1], pass_forms[2])


def inverse_of(kernel, spec_real, spec_imag, tables):
    weight = kernel[..., None]
    real_part = (weight * spec_real).astype(jnp.bfloat16)
    imag_part = (weight * spec_imag).astype(jnp.bfloat16)
    real_part, imag_part = complex_pass(real_part, imag_part, tables[2], tables[3], pass_forms[0])
    real_part, imag_part = complex_pass(real_part, imag_part, tables[2], tables[3], pass_forms[1])
    return last_pass(real_part, imag_part, tables[2], tables[3], pass_forms[2])


def collide(moved_block, kern_first, kern_second, kern_loss, tables):
    rounded = moved_block.astype(jnp.bfloat16)
    spec_real, spec_imag = spectrum_of(rounded, tables)

    def add_direction(direction, running):
        return running + inverse_of(kern_first[direction], spec_real, spec_imag, tables) * inverse_of(kern_second[direction], spec_real, spec_imag, tables)

    gain = lax.fori_loop(0, kern_first.shape[0], add_direction, jnp.zeros(moved_block.shape, jnp.float32))
    return gain - moved_block * inverse_of(kern_loss, spec_real, spec_imag, tables)


def transport(padded, along_x, along_y):
    center = padded[1:-1, 1:-1]
    back_x = center - padded[:-2, 1:-1]
    front_x = padded[2:, 1:-1] - center
    back_y = center - padded[1:-1, :-2]
    front_y = padded[1:-1, 2:] - center
    plus_x = jnp.maximum(along_x, 0.0)[None, None, :]
    minus_x = jnp.minimum(along_x, 0.0)[None, None, :]
    plus_y = jnp.maximum(along_y, 0.0)[None, None, :]
    minus_y = jnp.minimum(along_y, 0.0)[None, None, :]
    return -courant * (plus_x * back_x + minus_x * front_x + plus_y * back_y + minus_y * front_y)


def reference(distribution, cell_type, first_kernel, second_kernel, loss_kernel):
    vel_count = NVEL ** 3
    along_x, along_y, along_z = components(NVEL)
    still_wall, moving = wall_tables(along_x, along_y, along_z)
    density = jnp.sum(distribution, axis=2)
    fluid_cell_mask = cell_type == 0
    thermal = density[:, :, None] * jnp.where(cell_type[:, :, None] == 1, still_wall[None, None, :], moving[None, None, :])
    walled = jnp.where(fluid_cell_mask[:, :, None], distribution, thermal)
    padded = jnp.pad(walled, ((1, 1), (1, 1), (0, 0)))
    increment = transport(padded, along_x, along_y)
    advected_state = jnp.where(fluid_cell_mask[:, :, None], walled + increment, walled)
    tables = fourier_tables(NVEL)
    block_size = SLAB * CY
    block_count = N_VEL * N_CELL
    blocks = advected_state.reshape(N_VEL, SLAB, N_CELL, CY, vel_count).transpose(0, 2, 4, 1, 3)
    blocks = blocks.reshape(block_count, NVEL, NVEL, NVEL, block_size)
    kern_first = first_kernel.reshape(DIRS, NVEL, NVEL, NVEL)
    kern_second = second_kernel.reshape(DIRS, NVEL, NVEL, NVEL)
    kern_loss = loss_kernel.reshape(NVEL, NVEL, NVEL)

    def one_block(cell_piece):
        return collide(cell_piece, kern_first, kern_second, kern_loss, tables)

    result = lax.map(one_block, blocks)
    collision_operator = result.reshape(N_VEL, N_CELL, vel_count, SLAB, CY).transpose(0, 3, 1, 4, 2).reshape(NX, NY, vel_count)
    return jnp.where(fluid_cell_mask[:, :, None], advected_state + collision_timestep * collision_operator, advected_state)
```

```python
import functools
import math

import jax
import jax.numpy as jnp
import numpy as np
from jax import lax
from jax.experimental import pallas as pl
from jax.experimental.pallas import tpu as pltpu
from jax.sharding import PartitionSpec as P

N = 16
HALF = N // 2
PLANE = N * N
TILE = N * HALF
CELLS = 8
CHUNKS = 4
UNROLL = 16
courant = 0.45
collision_timestep = 0.1
bf16 = jnp.bfloat16
f32 = jnp.float32


def velocity_tables():
    levels = ((2.0 * np.arange(N, dtype=np.float32) - (N - 1)) / (N - 1)).astype(np.float64)
    cx = np.repeat(levels, PLANE)
    cy = np.tile(np.repeat(levels, N), N)
    cz = np.tile(levels, PLANE)
    still = np.exp(-4.5 * (cx * cx + cy * cy + cz * cz))
    moving = np.exp(-0.5 * ((3.0 * cx - 1.0) ** 2 + 9.0 * cy * cy + 9.0 * cz * cz))
    zero = np.zeros_like(cx)
    rows = [np.maximum(cx, 0), np.minimum(cx, 0), np.maximum(cy, 0), np.minimum(cy, 0),
            still / still.sum(), moving / moving.sum(), zero, zero]
    return np.stack(rows).astype(np.float32)


def fourier_matrices():
    n = np.arange(N)
    angles = 2.0 * math.pi * ((n[:, None] * n[None, :]) % N) / N
    rounded = lambda t: t.astype(np.float32).astype(jnp.bfloat16).astype(np.float64)
    c, s = rounded(np.cos(angles)), rounded(np.sin(angles))
    by_cell, by_line = np.eye(CELLS), np.eye(N)
    forward_i = np.concatenate([np.kron(c, by_cell), np.kron(-s, by_cell)], 0)
    cj, sj = np.kron(c, by_line), np.kron(s, by_line)
    forward_j = np.block([[cj, -sj], [sj, cj]])
    ck, sk = np.kron(by_line, c), np.kron(by_line, s)
    whole = np.block([[ck, -sk], [sk, ck]]).reshape(2 * PLANE, 2, N, N)
    low = whole[..., :HALF]
    top = np.zeros_like(low)
    top[..., 0] = whole[..., HALF]
    forward_k = np.concatenate([low.reshape(2 * PLANE, PLANE), top.reshape(2 * PLANE, PLANE)], 1)
    turn = np.stack([np.stack([c, -s], -1), np.stack([s, c], -1)], 0) / N
    inverse_i = np.kron(turn.reshape(2 * N, 2 * N), by_cell)
    c, s = c / N, s / N
    spread = lambda left, right: np.einsum("bj,d->jbd", left, right)
    last = np.zeros((2, N, HALF, N, N))
    for k in range(1, HALF):
        last[0, :, k] = 2.0 * (spread(c, c[:, k]) - spread(s, s[:, k]))
        last[1, :, k] = -2.0 * (spread(c, s[:, k]) + spread(s, c[:, k]))
    last[0, :, 0] = spread(c, c[:, 0]) + spread(s, c[:, HALF])
    last[1, :, 0] = spread(c, c[:, HALF]) - spread(s, c[:, 0])
    inverse_jk = last.reshape(PLANE, PLANE)
    return [t.astype(np.float32).astype(jnp.bfloat16) for t in (forward_i, forward_j, forward_k, inverse_i, inverse_jk)]


def half_selection():
    eye = np.eye(PLANE, dtype=np.float32).reshape(PLANE, N, N)
    low = eye[..., :HALF]
    top = np.zeros_like(low)
    top[..., 0] = eye[..., HALF]
    straight = np.concatenate([low.reshape(PLANE, TILE), top.reshape(PLANE, TILE)], 1)
    flip = (-np.arange(N)) % N
    mirrored = straight.reshape(N, N, PLANE)[flip][:, flip].reshape(PLANE, PLANE)
    return np.concatenate([straight, mirrored], 1).astype(jnp.bfloat16)


def dot(left, right):
    return jnp.dot(left, right, preferred_element_type=f32)


def call(kernel, out_shape, operands, flops=0, scratch=(), **options):
    moved = sum(a.size * a.dtype.itemsize for a in list(operands) + jax.tree.leaves(out_shape))
    return pl.pallas_call(
        kernel, out_shape=out_shape, scratch_shapes=list(scratch),
        compiler_params=pltpu.CompilerParams(vmem_limit_bytes=40 * 2 ** 20),
        cost_estimate=pl.CostEstimate(flops=flops, bytes_accessed=moved, transcendentals=0),
        **options,
    )(*operands)


def kernels_body(first_ref, second_ref, loss_ref, pick_ref, low_ref, top_ref):
    pick = pick_ref[...]
    start = 0
    for source in (first_ref, second_ref, loss_ref):
        count = source.shape[0]
        picked = []
        for i in range(N):
            value = source[:, PLANE * i:PLANE * (i + 1)]
            total = 0.0
            for _ in range(3):
                part = value.astype(bf16)
                value = value - part.astype(f32)
                total = total + dot(part, pick)
            picked.append(total)
        for i in range(N):
            here, there = picked[i], picked[-i % N]
            even = 0.5 * (here[:, :PLANE] + there[:, PLANE:])
            low_ref[i, start:start + count, :] = even[:, :TILE]
            top_ref[i, start:start + count, :] = even[:, TILE:]
        start += count


def half_kernels(first_kernel, second_kernel, loss_kernel):
    total = first_kernel.shape[0] + second_kernel.shape[0] + 1
    shape = jax.ShapeDtypeStruct((N, total, TILE), f32)
    operands = (first_kernel, second_kernel, loss_kernel[None, :], jnp.asarray(half_selection()))
    return call(kernels_body, (shape, shape), operands, flops=6 * total * N * PLANE * 2 * PLANE)


def column_of(table, lane, row):
    return jnp.sum(jnp.where(lane == row, table, 0.0), axis=1, keepdims=True)


def density_body(cells_ref, sum_ref):
    rows, cols, _ = cells_ref.shape
    lane = lax.broadcasted_iota(jnp.int32, (cols, rows), 1)

    def add(row, total):
        return jnp.where(lane == row, jnp.sum(cells_ref[row], axis=1, keepdims=True), total)

    sum_ref[...] = lax.fori_loop(0, rows, add, jnp.zeros((cols, rows), f32), unroll=8)


def walled_row(cells_ref, kind, density, tables_ref, lane, row):
    here = column_of(kind, lane, row)
    wall = jnp.where(here == 1.0, tables_ref[4:5, :], tables_ref[5:6, :]) * column_of(density, lane, row)
    return jnp.where(here == 0.0, cells_ref[row], wall), here


def rim_body(groups, *refs):
    cells_ref, kind_ref, tables_ref = refs[:3]
    sums = refs[3:3 + groups]
    density_ref, first_ref, last_ref = refs[3 + groups:]
    rows, cols, width = cells_ref.shape
    density = sums[0][...]
    for other in sums[1:]:
        density = density + other[...]
    density_ref[...] = density
    kind = kind_ref[...]
    lane = lax.broadcasted_iota(jnp.int32, (cols, rows), 1)

    def one_row(row, _):
        walled, _ = walled_row(cells_ref, kind, density, tables_ref, lane, row)
        for block in range(width // PLANE):
            to = slice(TILE * block, TILE * (block + 1))
            at = PLANE * block
            first_ref[row, :, to] = walled[:1, at:at + TILE]
            last_ref[row, :, to] = walled[cols - 1:, at + TILE:at + PLANE]
        return 0

    lax.fori_loop(0, rows, one_row, 0, unroll=4)


def transport_body(groups, chunks, rank_ref, cells_ref, kind_ref, tables_ref, density_ref, before_ref, after_ref, *outs):
    rows, cols, width = cells_ref.shape
    per_chunk = rows // groups // chunks
    rank = rank_ref[0]
    kind, density = kind_ref[...], density_ref[...]
    lane = lax.broadcasted_iota(jnp.int32, (cols, rows), 1)
    sub = lax.broadcasted_iota(jnp.int32, (cols, TILE), 0)
    row_of = lambda row: walled_row(cells_ref, kind, density, tables_ref, lane, row)
    for chunk in range(chunks):
        for flip in range(groups):
            out_ref = outs[chunk * groups + flip]
            top = lax.bitwise_xor(rank, flip) * (rows // groups) + chunk * per_chunk

            def one_row(step, carry):
                past, here, kind_here = carry
                row = top + step
                ahead, kind_ahead = row_of(jnp.minimum(row + 1, rows - 1))
                back_x = here - past
                front_x = ahead - here
                parts = []
                for tile in range(width // TILE):
                    at = slice(TILE * tile, TILE * (tile + 1))
                    rim = slice(TILE * (tile // 2), TILE * (tile // 2 + 1))
                    now = here[:, at]
                    drift = tables_ref[0:1, at] * back_x[:, at] + tables_ref[1:2, at] * front_x[:, at]
                    if tile % 2:
                        near = jnp.where(sub == 0, before_ref[row, :, rim], pltpu.roll(now, 1, 0))
                        drift = drift + tables_ref[2:3, at] * (now - near)
                    else:
                        near = jnp.where(sub == cols - 1, after_ref[row, :, rim], pltpu.roll(now, cols - 1, 0))
                        drift = drift + tables_ref[3:4, at] * (near - now)
                    out_ref[step, :, at] = jnp.where(kind_here == 0.0, now + -courant * drift, now)
                return here, ahead, kind_ahead

            start = row_of(jnp.maximum(top - 1, 0))[0], *row_of(top)
            lax.fori_loop(0, per_chunk, one_row, start)


def collide_body(groups, dirs, *refs):
    rank_ref = refs[0]
    sources = refs[1:1 + groups]
    kind_ref, low_ref, top_ref, fi_ref, fj_ref, fk_ref, ii_ref, ijk_ref = refs[1 + groups:9 + groups]
    outs = refs[9 + groups:9 + 2 * groups]
    moved_ref, spec_ref, gain_ref = refs[9 + 2 * groups:]
    rows = N * CELLS
    per = N // groups
    rank = rank_ref[0]
    for flip, source in enumerate(sources):
        at = lax.bitwise_xor(rank, flip) * per
        for i in range(per):
            moved_ref[at + i] = source[0, :, PLANE * i:PLANE * (i + 1)]
    moved = moved_ref[...].reshape(rows, PLANE)
    value = dot(fi_ref[...], moved.astype(bf16)).astype(bf16)
    value = jnp.concatenate([value[:rows], value[rows:]], 1)
    value = dot(value, fj_ref[...]).astype(bf16)
    spec_ref[...] = dot(value, fk_ref[...]).astype(bf16).astype(f32)

    def weighted(p):
        parts = []
        for i in range(N):
            at = slice(CELLS * i, CELLS * (i + 1))
            low_re, low_im, top_re, top_im = (spec_ref[at, TILE * t:TILE * (t + 1)] for t in range(4))
            low, top = low_ref[i, p:p + 1, :], top_ref[i, p:p + 1, :]
            parts.append(low * low_re - top * top_im)
            parts.append(low * low_im + top * top_re)
        return jnp.concatenate(parts, 0).astype(bf16)

    def back(one, other):
        value = dot(ii_ref[...], jnp.concatenate([weighted(one), weighted(other)], 1)).astype(bf16)
        value = jnp.concatenate([
            jnp.concatenate([value[:rows, :TILE], value[rows:, :TILE]], 1),
            jnp.concatenate([value[:rows, TILE:], value[rows:, TILE:]], 1)], 0)
        value = dot(value, ijk_ref[...])
        return value[:rows], value[rows:]

    loss, other = back(2 * dirs, 0)
    gain_ref[...] = -moved * loss
    for p in range(dirs):
        one, other = back(p, dirs + p)
        gain_ref[...] += one * other
    fluid = kind_ref[0] == 0.0
    now = moved_ref[...]
    updated = jnp.where(fluid, now + collision_timestep * gain_ref[...].reshape(N, CELLS, PLANE), now)
    moved_ref[...] = updated
    for flip, out_ref in enumerate(outs):
        at = lax.bitwise_xor(rank, flip) * per
        for i in range(per):
            out_ref[0, :, PLANE * i:PLANE * (i + 1)] = moved_ref[at + i]


def collide(rank, blocks, kinds, low, top):
    groups = len(blocks)
    dirs = low.shape[1] // 2
    steps, cols, width = blocks[0].shape
    tables = [jnp.asarray(m) for m in fourier_matrices()]
    block = pl.BlockSpec((1, cols, width), lambda g: (g, 0, 0))
    whole = lambda a: pl.BlockSpec(a.shape, lambda g: (0,) * a.ndim)
    shape = jax.ShapeDtypeStruct(blocks[0].shape, f32)
    return call(
        functools.partial(collide_body, groups, dirs), (shape,) * groups,
        (rank, *blocks, kinds, low, top, *tables),
        flops=steps * 2 * PLANE ** 3 * (2 * dirs + 6),
        scratch=[pltpu.VMEM((N, CELLS, PLANE), f32), pltpu.VMEM((N * CELLS, 2 * PLANE), f32), pltpu.VMEM((N * CELLS, PLANE), f32)],
        grid=(steps,),
        in_specs=[pl.BlockSpec(memory_space=pltpu.SMEM)] + [block] * groups
        + [pl.BlockSpec((1, cols, 1), lambda g: (g, 0, 0))] + [whole(a) for a in (low, top, *tables)],
        out_specs=(block,) * groups,
    )


def on_device(distribution, cell_type, first_kernel, second_kernel, loss_kernel):
    rows, cols, width = distribution.shape
    groups = lax.axis_size("vel")
    rank = lax.axis_index("vel")
    spots = lax.axis_size("cell")
    own_rows = rows // groups
    per_chunk = own_rows // CHUNKS
    rank_word = rank.astype(jnp.int32)[None]
    tables = lax.dynamic_slice_in_dim(jnp.asarray(velocity_tables()), rank * width, width, 1)
    kind = cell_type.astype(f32)
    kind_by_col = kind.T
    own_kind = lax.dynamic_slice_in_dim(kind, rank * own_rows, own_rows, 0)[:, :, None]

    def swap(value, flip):
        return lax.ppermute(value, "vel", [(i, i ^ flip) for i in range(groups)])

    partial = call(density_body, jax.ShapeDtypeStruct((cols, rows), f32), (distribution,))
    sums = [partial] + [swap(partial, flip) for flip in range(1, groups)]
    low, top = half_kernels(first_kernel, second_kernel, loss_kernel)
    rim = jax.ShapeDtypeStruct((rows, 1, width // 2), f32)
    density, first, last = call(
        functools.partial(rim_body, groups), (jax.ShapeDtypeStruct((cols, rows), f32), rim, rim),
        (distribution, kind_by_col, tables, *sums))
    before = lax.ppermute(last, "cell", [(i, i + 1) for i in range(spots - 1)])
    after = lax.ppermute(first, "cell", [(i + 1, i) for i in range(spots - 1)])
    vmem = pl.BlockSpec(memory_space=pltpu.VMEM)
    piece = jax.ShapeDtypeStruct((per_chunk, cols, width), f32)
    pieces = call(
        functools.partial(transport_body, groups, CHUNKS), (piece,) * (CHUNKS * groups),
        (rank_word, distribution, kind_by_col, tables, density, before, after),
        in_specs=[pl.BlockSpec(memory_space=pltpu.SMEM)] + [vmem] * 6, out_specs=(vmem,) * (CHUNKS * groups))
    updated = jnp.zeros((rows, cols, width), f32)
    arrived = []
    for chunk in range(CHUNKS):
        mine = pieces[chunk * groups:(chunk + 1) * groups]
        arrived.append([mine[0]] + [swap(mine[flip], flip) for flip in range(1, groups)])
    for chunk in range(CHUNKS):
        done = collide(rank_word, arrived[chunk], own_kind[chunk * per_chunk:(chunk + 1) * per_chunk], low, top)
        for flip in range(groups):
            home = done[0] if flip == 0 else swap(done[flip], flip)
            updated = lax.dynamic_update_slice_in_dim(updated, home, (rank ^ flip) * own_rows + chunk * per_chunk, 0)
    return updated


def solution(mesh):
    return jax.shard_map(
        on_device,
        mesh=mesh,
        in_specs=(P(None, "cell", "vel"), P(None, "cell"), P(), P(), P()),
        out_specs=P(None, "cell", "vel"),
        check_vma=False,
    )
```

```python
import functools
import math

import jax
import jax.numpy as jnp
import numpy as np
from jax import lax
from jax.experimental import pallas as pl
from jax.experimental.pallas import tpu as pltpu
from jax.sharding import PartitionSpec as P

N = 16
HALF = N // 2
PLANE = N * N
TILE = N * HALF
CELLS = 8
courant = 0.45
collision_timestep = 0.1
bf16 = jnp.bfloat16
f32 = jnp.float32


def velocity_tables():
    levels = ((2.0 * np.arange(N, dtype=np.float32) - (N - 1)) / (N - 1)).astype(np.float64)
    cx = np.repeat(levels, PLANE)
    cy = np.tile(np.repeat(levels, N), N)
    cz = np.tile(levels, PLANE)
    still = np.exp(-4.5 * (cx * cx + cy * cy + cz * cz))
    moving = np.exp(-0.5 * ((3.0 * cx - 1.0) ** 2 + 9.0 * cy * cy + 9.0 * cz * cz))
    rows = [np.abs(cx), np.abs(cy), still / still.sum(), moving / moving.sum()]
    rows += [np.zeros_like(cx)] * (8 - len(rows))
    return np.stack(rows).astype(np.float32).reshape(8, N, PLANE).transpose(1, 0, 2)


def fourier_matrices():
    n = np.arange(N)
    angles = 2.0 * math.pi * ((n[:, None] * n[None, :]) % N) / N
    rounded = lambda t: t.astype(np.float32).astype(jnp.bfloat16).astype(np.float64)
    c, s = rounded(np.cos(angles)), rounded(np.sin(angles))
    by_cell, by_line = np.eye(CELLS), np.eye(N)
    forward_i = np.concatenate([np.kron(c, by_cell), np.kron(-s, by_cell)], 0)
    cj, sj = np.kron(c, by_line), np.kron(s, by_line)
    pick = half_selection()[:, :PLANE]
    ck, sk = np.kron(by_line, c) @ pick, np.kron(by_line, s) @ pick
    turn = np.stack([np.stack([c, -s], -1), np.stack([s, c], -1)], 0) / N
    inverse_i = np.kron(turn.reshape(2 * N, 2 * N), by_cell)
    c, s = c / N, s / N
    spread = lambda left, right: np.einsum("bj,d->jbd", left, right)
    last = np.zeros((2, N, HALF, N, N))
    for k in range(1, HALF):
        last[0, :, k] = 2.0 * (spread(c, c[:, k]) - spread(s, s[:, k]))
        last[1, :, k] = -2.0 * (spread(c, s[:, k]) + spread(s, c[:, k]))
    last[0, :, 0] = spread(c, c[:, 0]) + spread(s, c[:, HALF])
    last[1, :, 0] = spread(c, c[:, HALF]) - spread(s, c[:, 0])
    inverse_jk = last.reshape(PLANE, PLANE)
    forward_i = np.concatenate([forward_i, np.zeros_like(forward_i)], 1)
    return np.stack([forward_i, cj, sj, ck, sk, inverse_i, inverse_jk]).astype(np.float32)


def half_selection():
    eye = np.eye(PLANE, dtype=np.float32).reshape(PLANE, N, N)
    low = eye[..., :HALF]
    top = np.zeros_like(low)
    top[..., 0] = eye[..., HALF]
    straight = np.concatenate([low.reshape(PLANE, TILE), top.reshape(PLANE, TILE)], 1)
    flip = (-np.arange(N)) % N
    mirrored = straight.reshape(N, N, PLANE)[flip][:, flip].reshape(PLANE, PLANE)
    return np.concatenate([straight, mirrored], 1)


def dot(left, right):
    return jnp.dot(left, right, preferred_element_type=f32)


def call(kernel, out_shape, operands, flops=0, scratch=(), limit=24, **options):
    moved = sum(a.size * a.dtype.itemsize for a in list(operands) + jax.tree.leaves(out_shape))
    return pl.pallas_call(
        kernel, out_shape=out_shape, scratch_shapes=list(scratch),
        compiler_params=pltpu.CompilerParams(vmem_limit_bytes=limit * 2 ** 20),
        cost_estimate=pl.CostEstimate(flops=flops, bytes_accessed=moved, transcendentals=0),
        **options,
    )(*operands)


def setup_body(first_ref, second_ref, loss_ref, pick_ref, table_ref, low_ref, top_ref, matrix_ref):
    dirs = first_ref.shape[0]
    matrix_ref[...] = table_ref[...].astype(bf16)
    parts = []
    for i in range(N):
        at = slice(PLANE * i, PLANE * (i + 1))
        value = jnp.concatenate([first_ref[:, at], second_ref[:, at], jnp.broadcast_to(loss_ref[:, at], (dirs, PLANE))], 0)
        for _ in range(3):
            part = value.astype(bf16)
            value = value - part.astype(f32)
            parts.append(part)
    picked = dot(jnp.concatenate(parts, 0), pick_ref[...].astype(bf16)).reshape(N, 3, 3 * dirs, 2 * PLANE)
    picked = picked[:, 0] + picked[:, 1] + picked[:, 2]
    for i in range(N):
        even = 0.5 * (picked[i, :, :PLANE] + picked[-i % N, :, PLANE:])
        low_ref[i] = even[:, :TILE]
        top_ref[i] = even[:, TILE:]


def setup(first_kernel, second_kernel, loss_kernel):
    total = 3 * first_kernel.shape[0]
    shape = jax.ShapeDtypeStruct((N, total, TILE), f32)
    matrices = fourier_matrices()
    operands = (first_kernel, second_kernel, loss_kernel[None, :], jnp.asarray(half_selection()), jnp.asarray(matrices))
    return call(setup_body, (shape, shape, jax.ShapeDtypeStruct(matrices.shape, bf16)), operands,
                flops=6 * total * N * PLANE * 2 * PLANE)


def column_of(table, lane, row):
    return jnp.sum(jnp.where(lane == row, table, 0.0), axis=1, keepdims=True)


def walled(kind, density, raw, table, at):
    return jnp.where(kind == 0.0, raw, jnp.where(kind == 1.0, table[2:3, at], table[3:4, at]) * density)


def window(rank, own_rows, total_rows, first_row, count):
    return jnp.clip(rank * own_rows + first_row - 1, 0, total_rows - count - 2)


def columns_body(cells_ref, kind_ref, after_ref, first_ref, last_ref):
    del after_ref
    rows, cols, width = cells_ref.shape
    half = width // 2
    lane = lax.broadcasted_iota(jnp.int32, (cols, TILE), 1)
    place = lax.broadcasted_iota(jnp.int32, (cols, rows), 1)
    kinds = kind_ref[...]

    def one_row(row, _):
        values = cells_ref[row]
        total = jnp.sum(values, axis=1, keepdims=True)
        tail = jnp.where(lane == 0, total, jnp.where(lane == 1, column_of(kinds, place, row), 0.0))
        for block in range(width // PLANE):
            to = slice(TILE * block, TILE * (block + 1))
            at = PLANE * block
            first_ref[row, :, to] = values[:1, at:at + TILE]
            last_ref[row, :, to] = values[cols - 1:, at + TILE:at + PLANE]
        first_ref[row, :, half:] = tail[:1]
        last_ref[row, :, half:] = tail[cols - 1:]
        return 0

    lax.fori_loop(0, rows, one_row, 0, unroll=8)


def cut_body(groups, first_row, rank_ref, cells_ref, after_ref, *refs):
    del after_ref
    columns, outs, sems = refs[:-1 - groups], refs[-1 - groups:-1], refs[-1]
    rows = cells_ref.shape[0]
    extra = 2 if columns else 0
    copies = []
    for flip, out_ref in enumerate(outs):
        count = out_ref.shape[0] - extra
        taker = lax.bitwise_xor(rank_ref[0], flip)
        top = window(taker, rows // groups, rows, first_row, count - 2)
        copies.append(pltpu.make_async_copy(cells_ref.at[pl.ds(top, count)], out_ref.at[pl.ds(0, count)], sems.at[flip]))
    for copy in copies:
        copy.start()
    for flip, out_ref in enumerate(outs):
        count = out_ref.shape[0] - extra
        top = lax.bitwise_xor(rank_ref[0], flip) * (rows // groups) + first_row
        for side, column in enumerate(columns):
            half = column.shape[2] - TILE
            for step in range(count - 2):
                out_ref[count, step:step + 1, half * side:half * (side + 1)] = column[top + step, :, :half]
                out_ref[count + 1, step:step + 1, TILE * side:TILE * (side + 1)] = column[top + step, :, half:]
    for copy in copies:
        copy.wait()


def edges_body(groups, first_row, passing, rank_ref, *refs):
    sources, refs = refs[:groups], refs[groups:]
    kind_ref, tables_ref = refs[1:3]
    first_ref, last_ref, density_ref = refs[3 + passing:6 + passing]
    cols, total_rows = kind_ref.shape
    count = first_ref.shape[0] // N
    carried = sources[0].shape[0] > count + 2
    half = sources[0].shape[2] // 2
    per = N // groups
    rank = rank_ref[0]
    kinds = kind_ref[...]
    place = lax.broadcasted_iota(jnp.int32, kinds.shape, 1)
    lane = lax.broadcasted_iota(jnp.int32, density_ref.shape, 1)
    start = window(rank, total_rows // groups, total_rows, first_row, count)
    densities = jnp.zeros(density_ref.shape, f32)
    for step in range(count + 2):
        row = jnp.clip(rank * (total_rows // groups) + first_row - 1 + step, 0, total_rows - 1)
        values = [source[row - start] for source in sources]
        density = jnp.sum(sum(values), axis=1, keepdims=True)
        densities = jnp.where(lane == step, density, densities)
        if 0 < step <= count:
            kind = column_of(kinds, place, row)
            at = slice(step - 1, step)
            tails = [[source[count + 3, at, TILE * side:TILE * (side + 1)] for source in sources] for side in range(2) if carried]
            known = [(column_of(tail[0], lane[:1], 1), column_of(sum(tail), lane[:1], 0)) for tail in tails]
            for flip, (value, source) in enumerate(zip(values, sources)):
                for i in range(per):
                    at = lax.bitwise_xor(rank, flip) * per + i
                    table = tables_ref[at]
                    for tile, cell, out_ref in ((0, 0, first_ref), (1, cols - 1, last_ref)):
                        of = slice(TILE * tile, TILE * (tile + 1))
                        if carried:
                            raw = source[count + 2, step - 1:step, half * (1 - tile) + TILE * i:half * (1 - tile) + TILE * (i + 1)]
                            out_ref[(step - 1) * N + at] = walled(*known[1 - tile], raw, table, of)
                        else:
                            edge = walled(kind, density, value[:, PLANE * i + TILE * tile:PLANE * i + TILE * (tile + 1)], table, of)
                            out_ref[(step - 1) * N + at] = edge[cell:cell + 1]
    density_ref[...] = densities


def collide_body(groups, dirs, batch, first_row, rank_ref, *refs):
    sources, refs = refs[:groups], refs[groups:]
    before_ref, after_ref, density_ref, kind_ref, tables_ref, low_ref, top_ref, matrix_ref, _ = refs[:9]
    outs, refs = refs[9:9 + groups], refs[9 + groups:]
    moved_refs, spec_refs, gain_ref = refs[:2], refs[2:4], refs[4]
    rows = N * CELLS
    per = N // groups
    steps = outs[0].shape[0]
    total_rows = kind_ref.shape[1]
    own_rows = total_rows // groups
    rank = rank_ref[0]
    sub = lax.broadcasted_iota(jnp.int32, (CELLS, TILE), 0)
    place = lax.broadcasted_iota(jnp.int32, kind_ref.shape, 1)
    lane = lax.broadcasted_iota(jnp.int32, density_ref.shape, 1)
    kinds, densities = kind_ref[...], density_ref[...]
    origin = rank * own_rows + first_row
    start = window(rank, own_rows, total_rows, first_row, steps)

    def cells_of(step):
        row = jnp.clip(origin + step, 0, total_rows - 1)
        return row - start, column_of(kinds, place, row), column_of(densities, lane, step + 1)

    def turned(value, at):
        straight, crossed = dot(value, matrix_ref[at]), dot(value, matrix_ref[at + 1])
        return jnp.concatenate([straight[:rows] + crossed[rows:], straight[rows:] - crossed[:rows]], 0)

    def prepare(step, moved_ref, spec_ref):
        now_at, kind, density = cells_of(step)
        past, ahead = cells_of(step - 1), cells_of(step + 1)
        for flip, source in enumerate(sources):
            owner = lax.bitwise_xor(rank, flip)
            positive = owner >= groups // 2
            other_at, other_kind, other_density = (jnp.where(positive, p, a) for p, a in zip(past, ahead))
            for i in range(per):
                line = owner * per + i
                table = tables_ref[line]
                for tile in range(2):
                    at = slice(TILE * tile, TILE * (tile + 1))
                    of = slice(PLANE * i + TILE * tile, PLANE * i + TILE * (tile + 1))
                    now = walled(kind, density, source[now_at, :, of], table, at)
                    other = walled(other_kind, other_density, source[other_at, :, of], table, at)
                    if tile:
                        near = jnp.where(sub == 0, before_ref[step * N + line], pltpu.roll(now, 1, 0))
                    else:
                        near = jnp.where(sub == CELLS - 1, after_ref[step * N + line], pltpu.roll(now, CELLS - 1, 0))
                    drift = table[0:1, at] * (now - other) + table[1:2, at] * (now - near)
                    moved_ref[line, :, at] = jnp.where(kind == 0.0, now - courant * drift, now)
        yield
        value = dot(matrix_ref[0, :, :rows], moved_ref[...].reshape(rows, PLANE).astype(bf16)).astype(bf16)
        yield
        value = turned(value, 1).astype(bf16)
        yield
        spec_ref[...] = turned(value, 3).astype(bf16).astype(f32)
        yield

    def finish(step, moved_ref, spec_ref, beside):
        def weighted(*pair):
            parts = [[] for _ in pair]
            for i in range(N):
                re_at, im_at = slice(CELLS * i, CELLS * (i + 1)), slice(rows + CELLS * i, rows + CELLS * (i + 1))
                low_re, top_re = spec_ref[re_at, :TILE], spec_ref[re_at, TILE:]
                low_im, top_im = spec_ref[im_at, :TILE], spec_ref[im_at, TILE:]
                for p, part in zip(pair, parts):
                    low, top = low_ref[i, p:p + 1, :], top_ref[i, p:p + 1, :]
                    part.append(low * low_re - top * top_im)
                    part.append(low * low_im + top * top_re)
            return jnp.concatenate([jnp.concatenate(part, 0) for part in parts], 1).astype(bf16)

        def along_i(*pair):
            value = dot(matrix_ref[5], weighted(*pair)).astype(bf16)
            return [jnp.concatenate([value[:rows, TILE * t:TILE * (t + 1)], value[rows:, TILE * t:TILE * (t + 1)]], 1)
                    for t in range(len(pair))]

        gain_ref[...] = jnp.zeros_like(gain_ref)
        for first in range(0, dirs, batch):
            stack = []
            for p in range(first, min(first + batch, dirs)):
                stack += along_i(p, dirs + p)
            value = dot(jnp.concatenate(stack, 0), matrix_ref[6])
            total = gain_ref[...]
            for at in range(0, value.shape[0], 2 * rows):
                total = total + value[at:at + rows] * value[at + rows:at + 2 * rows]
            gain_ref[...] = total
            next(beside, None)
        for _ in beside:
            pass
        loss = dot(along_i(2 * dirs)[0], matrix_ref[6])
        now = moved_ref[...]
        collision = (gain_ref[...] - now.reshape(rows, PLANE) * loss).reshape(N, CELLS, PLANE)
        moved_ref[...] = jnp.where(cells_of(step)[1] == 0.0, now + collision_timestep * collision, now)
        for flip, out_ref in enumerate(outs):
            at = lax.bitwise_xor(rank, flip) * per
            for i in range(per):
                out_ref[step, :, PLANE * i:PLANE * (i + 1)] = moved_ref[at + i]

    for _ in prepare(0, moved_refs[0], spec_refs[0]):
        pass

    def two_rows(pair, _):
        one, other = 2 * pair, jnp.minimum(2 * pair + 1, steps - 1)
        following = jnp.minimum(2 * pair + 2, steps - 1)
        finish(one, moved_refs[0], spec_refs[0], prepare(other, moved_refs[1], spec_refs[1]))
        finish(other, moved_refs[1], spec_refs[1], prepare(following, moved_refs[0], spec_refs[0]))
        return 0

    lax.fori_loop(0, (steps + 1) // 2, two_rows, 0)


def collide(rank, sources, before, after, density, kinds, tables, low, top, matrices, earlier, first_row, steps):
    groups = len(sources)
    dirs = low.shape[1] // 3
    _, cols, width = sources[0].shape
    vmem = pl.BlockSpec(memory_space=pltpu.VMEM)
    shape = jax.ShapeDtypeStruct((steps, cols, width), f32)
    operands = (*sources, before, after, density, kinds, tables, low, top, matrices, earlier)
    cells = pltpu.VMEM((N, CELLS, PLANE), f32)
    spec = pltpu.VMEM((2 * N * CELLS, PLANE), f32)
    return call(
        functools.partial(collide_body, groups, dirs, 4, first_row), (shape,) * groups, (rank, *operands),
        flops=steps * 2 * PLANE ** 3 * (2 * dirs + 6),
        scratch=[cells, cells, spec, spec, pltpu.VMEM((N * CELLS, PLANE), f32)],
        in_specs=[pl.BlockSpec(memory_space=pltpu.SMEM)] + [vmem] * (len(operands) - 1) + [pl.BlockSpec(memory_space=pl.ANY)],
        out_specs=(vmem,) * groups,
    )


def on_device(distribution, cell_type, first_kernel, second_kernel, loss_kernel):
    rows, cols, width = distribution.shape
    groups = lax.axis_size("vel")
    rank = lax.axis_index("vel")
    spots = lax.axis_size("cell")
    own_rows = rows // groups
    half = (own_rows // 4) * 2
    chunks = [(0, half), (half, own_rows - half)]
    rank_word = rank.astype(jnp.int32)[None]
    tables = jnp.asarray(velocity_tables())
    kinds = cell_type.astype(f32).T
    vmem = pl.BlockSpec(memory_space=pltpu.VMEM)
    smem = pl.BlockSpec(memory_space=pltpu.SMEM)
    anywhere = pl.BlockSpec(memory_space=pl.ANY)

    def swap(values):
        swapped = {0: values[0]}
        for flip in reversed(range(1, groups)):
            swapped[flip] = lax.ppermute(values[flip], "vel", [(i, i ^ flip) for i in range(groups)])
        return [swapped[flip] for flip in range(groups)]

    def cut(first_row, count, earlier, *columns):
        block = jax.ShapeDtypeStruct((count + 2 + len(columns), cols, width), f32)
        place = vmem
        return call(
            functools.partial(cut_body, groups, first_row), (block,) * groups, (rank_word, distribution, earlier, *columns),
            in_specs=[smem, anywhere, anywhere] + [vmem] * len(columns), out_specs=(place,) * groups,
            scratch=[pltpu.SemaphoreType.DMA((groups,))], limit=24 if columns else 52)

    def rims(first_row, count, sources, *passing):
        edge = jax.ShapeDtypeStruct((count * N, 1, TILE), f32)
        same = [jax.ShapeDtypeStruct(value.shape, f32) for value in passing]
        return call(
            functools.partial(edges_body, groups, first_row, len(passing)),
            (edge, edge, jax.ShapeDtypeStruct((cols, TILE), f32), *same),
            (rank_word, *sources, matrices, kinds, tables, *passing),
            in_specs=[smem] + [vmem] * groups + [anywhere, vmem, vmem] + [anywhere] * len(passing),
            out_specs=(vmem,) * 3 + (anywhere,) * len(passing),
            input_output_aliases={groups + 4 + at: 3 + at for at in range(len(passing))})

    def to_neighbours(first, last):
        return (lax.ppermute(last, "cell", [(i, i + 1) for i in range(spots - 1)]),
                lax.ppermute(first, "cell", [(i + 1, i) for i in range(spots - 1)]))

    (first_row, count), (next_row, next_count) = chunks
    cuts = cut(first_row, count, rank_word)
    sources = swap(cuts)
    low, top, matrices = setup(first_kernel, second_kernel, loss_kernel)
    column = jax.ShapeDtypeStruct((rows, 1, width // 2 + TILE), f32)
    columns = to_neighbours(*call(
        columns_body, (column, column), (distribution, kinds, cuts[0]), in_specs=[vmem, vmem, anywhere], out_specs=(vmem,) * 2))
    first, last, density = rims(first_row, count, sources)
    edges = to_neighbours(first, last)
    following = cut(next_row, next_count, sources[-1], *columns)
    done = collide(rank_word, sources, *edges, density, kinds, tables, low, top, matrices, following[0], first_row, count)
    sources = swap(following)
    after, before, density, *done = rims(next_row, next_count, sources, *done)
    home = swap(done)
    done = collide(rank_word, sources, before, after, density, kinds, tables, low, top, matrices, done[0], next_row, next_count)
    home = [home, swap(done)]
    updated = jnp.zeros((rows, cols, width), f32)
    for (first_row, count), blocks in zip(chunks, home):
        for flip, block in enumerate(blocks):
            updated = lax.dynamic_update_slice_in_dim(updated, block, (rank ^ flip) * own_rows + first_row, 0)
    return updated


def solution(mesh):
    return jax.shard_map(
        on_device,
        mesh=mesh,
        in_specs=(P(None, "cell", "vel"), P(None, "cell"), P(), P(), P()),
        out_specs=P(None, "cell", "vel"),
        check_vma=False,
    )
```

```python
import functools
import math

import jax
import jax.numpy as jnp
import numpy as np
from jax import lax
from jax.experimental import pallas as pl
from jax.experimental.pallas import tpu as pltpu
from jax.sharding import PartitionSpec as P

N = 16
HALF = N // 2
PLANE = N * N
TILE = N * HALF
CELLS = 8
courant = 0.45
collision_timestep = 0.1
bf16 = jnp.bfloat16
f32 = jnp.float32


def velocity_tables():
    levels = ((2.0 * np.arange(N, dtype=np.float32) - (N - 1)) / (N - 1)).astype(np.float64)
    cx = np.repeat(levels, PLANE)
    cy = np.tile(np.repeat(levels, N), N)
    cz = np.tile(levels, PLANE)
    still = np.exp(-4.5 * (cx * cx + cy * cy + cz * cz))
    moving = np.exp(-0.5 * ((3.0 * cx - 1.0) ** 2 + 9.0 * cy * cy + 9.0 * cz * cz))
    rows = [np.abs(cx), np.abs(cy), still / still.sum(), moving / moving.sum()]
    rows += [np.zeros_like(cx)] * (8 - len(rows))
    return np.stack(rows).astype(np.float32).reshape(8, N, PLANE).transpose(1, 0, 2)


def fourier_matrices():
    n = np.arange(N)
    angles = 2.0 * math.pi * ((n[:, None] * n[None, :]) % N) / N
    rounded = lambda t: t.astype(np.float32).astype(jnp.bfloat16).astype(np.float64)
    c, s = rounded(np.cos(angles)), rounded(np.sin(angles))
    by_cell, by_line = np.eye(CELLS), np.eye(N)
    forward_i = np.concatenate([np.kron(c, by_cell), np.kron(-s, by_cell)], 0)
    cj, sj = np.kron(c, by_line), np.kron(s, by_line)
    pick = half_selection()[:, :PLANE]
    ck, sk = np.kron(by_line, c) @ pick, np.kron(by_line, s) @ pick
    turn = np.stack([np.stack([c, -s], -1), np.stack([s, c], -1)], 0) / N
    inverse_i = np.kron(turn.reshape(2 * N, 2 * N), by_cell)
    c, s = c / N, s / N
    spread = lambda left, right: np.einsum("bj,d->jbd", left, right)
    last = np.zeros((2, N, HALF, N, N))
    for k in range(1, HALF):
        last[0, :, k] = 2.0 * (spread(c, c[:, k]) - spread(s, s[:, k]))
        last[1, :, k] = -2.0 * (spread(c, s[:, k]) + spread(s, c[:, k]))
    last[0, :, 0] = spread(c, c[:, 0]) + spread(s, c[:, HALF])
    last[1, :, 0] = spread(c, c[:, HALF]) - spread(s, c[:, 0])
    inverse_jk = last.reshape(PLANE, PLANE)
    forward_i = np.concatenate([forward_i, np.zeros_like(forward_i)], 1)
    return np.stack([forward_i, cj, sj, ck, sk, inverse_i, inverse_jk]).astype(np.float32)


def half_selection():
    eye = np.eye(PLANE, dtype=np.float32).reshape(PLANE, N, N)
    low = eye[..., :HALF]
    top = np.zeros_like(low)
    top[..., 0] = eye[..., HALF]
    straight = np.concatenate([low.reshape(PLANE, TILE), top.reshape(PLANE, TILE)], 1)
    flip = (-np.arange(N)) % N
    mirrored = straight.reshape(N, N, PLANE)[flip][:, flip].reshape(PLANE, PLANE)
    return np.concatenate([straight, mirrored], 1)


def dot(left, right):
    return jnp.dot(left, right, preferred_element_type=f32)


def call(kernel, out_shape, operands, flops=0, scratch=(), limit=2, **options):
    moved = sum(a.size * a.dtype.itemsize for a in list(operands) + jax.tree.leaves(out_shape))
    return pl.pallas_call(
        kernel, out_shape=out_shape, scratch_shapes=list(scratch),
        compiler_params=pltpu.CompilerParams(vmem_limit_bytes=limit * 2 ** 20),
        cost_estimate=pl.CostEstimate(flops=flops, bytes_accessed=moved, transcendentals=0),
        **options,
    )(*operands)


def setup_body(first_ref, second_ref, loss_ref, pick_ref, table_ref, low_ref, top_ref, matrix_ref):
    dirs = first_ref.shape[0]
    matrix_ref[...] = table_ref[...].astype(bf16)
    parts = []
    for i in range(N):
        at = slice(PLANE * i, PLANE * (i + 1))
        value = jnp.concatenate([first_ref[:, at], second_ref[:, at], jnp.broadcast_to(loss_ref[:, at], (dirs, PLANE))], 0)
        for _ in range(3):
            part = value.astype(bf16)
            value = value - part.astype(f32)
            parts.append(part)
    picked = dot(jnp.concatenate(parts, 0), pick_ref[...].astype(bf16)).reshape(N, 3, 3 * dirs, 2 * PLANE)
    picked = picked[:, 0] + picked[:, 1] + picked[:, 2]
    for i in range(N):
        even = 0.5 * (picked[i, :, :PLANE] + picked[-i % N, :, PLANE:])
        low_ref[i] = even[:, :TILE]
        top_ref[i] = even[:, TILE:]


def setup(first_kernel, second_kernel, loss_kernel):
    total = 3 * first_kernel.shape[0]
    shape = jax.ShapeDtypeStruct((N, total, TILE), f32)
    matrices = fourier_matrices()
    operands = (first_kernel, second_kernel, loss_kernel[None, :], jnp.asarray(half_selection()), jnp.asarray(matrices))
    return call(setup_body, (shape, shape, jax.ShapeDtypeStruct(matrices.shape, bf16)), operands,
                flops=6 * total * N * PLANE * 2 * PLANE)


def column_of(table, lane, row):
    return jnp.sum(jnp.where(lane == row, table, 0.0), axis=1, keepdims=True)


def walled(kind, density, raw, table, at):
    return jnp.where(kind == 0.0, raw, jnp.where(kind == 1.0, table[2:3, at], table[3:4, at]) * density)


def window(rank, own_rows, total_rows, first_row, count):
    return jnp.clip(rank * own_rows + first_row - 1, 0, total_rows - count - 2)


def columns_body(cells_ref, kind_ref, after_ref, first_ref, last_ref):
    del after_ref
    rows, cols, width = cells_ref.shape
    half = width // 2
    lane = lax.broadcasted_iota(jnp.int32, (cols, TILE), 1)
    place = lax.broadcasted_iota(jnp.int32, (cols, rows), 1)
    kinds = kind_ref[...]

    def one_row(row, _):
        values = cells_ref[row]
        total = jnp.sum(values, axis=1, keepdims=True)
        tail = jnp.where(lane == 0, total, jnp.where(lane == 1, column_of(kinds, place, row), 0.0))
        for block in range(width // PLANE):
            to = slice(TILE * block, TILE * (block + 1))
            at = PLANE * block
            first_ref[row, :, to] = values[:1, at:at + TILE]
            last_ref[row, :, to] = values[cols - 1:, at + TILE:at + PLANE]
        first_ref[row, :, half:] = tail[:1]
        last_ref[row, :, half:] = tail[cols - 1:]
        return 0

    lax.fori_loop(0, rows, one_row, 0, unroll=8)


def cut_body(groups, first_row, rank_ref, cells_ref, after_ref, *refs):
    del after_ref
    columns, outs, sems = refs[:-1 - groups], refs[-1 - groups:-1], refs[-1]
    rows = cells_ref.shape[0]
    extra = 2 if columns else 0
    copies = []
    for flip, out_ref in enumerate(outs):
        count = out_ref.shape[0] - extra
        taker = lax.bitwise_xor(rank_ref[0], flip)
        top = window(taker, rows // groups, rows, first_row, count - 2)
        copies.append(pltpu.make_async_copy(cells_ref.at[pl.ds(top, count)], out_ref.at[pl.ds(0, count)], sems.at[flip]))
    for copy in copies:
        copy.start()
    for flip, out_ref in enumerate(outs):
        count = out_ref.shape[0] - extra
        top = lax.bitwise_xor(rank_ref[0], flip) * (rows // groups) + first_row
        for side, column in enumerate(columns):
            half = column.shape[2] - TILE
            for step in range(count - 2):
                out_ref[count, step:step + 1, half * side:half * (side + 1)] = column[top + step, :, :half]
                out_ref[count + 1, step:step + 1, TILE * side:TILE * (side + 1)] = column[top + step, :, half:]
    for copy in copies:
        copy.wait()


def edges_body(groups, first_row, passing, rank_ref, *refs):
    sources, refs = refs[:groups], refs[groups:]
    kind_ref, tables_ref = refs[1:3]
    first_ref, last_ref, density_ref = refs[3 + passing:6 + passing]
    cols, total_rows = kind_ref.shape
    count = first_ref.shape[0] // N
    carried = sources[0].shape[0] > count + 2
    half = sources[0].shape[2] // 2
    per = N // groups
    rank = rank_ref[0]
    kinds = kind_ref[...]
    place = lax.broadcasted_iota(jnp.int32, kinds.shape, 1)
    lane = lax.broadcasted_iota(jnp.int32, density_ref.shape, 1)
    start = window(rank, total_rows // groups, total_rows, first_row, count)
    densities = jnp.zeros(density_ref.shape, f32)
    for step in range(count + 2):
        row = jnp.clip(rank * (total_rows // groups) + first_row - 1 + step, 0, total_rows - 1)
        values = [source[row - start] for source in sources]
        density = jnp.sum(sum(values), axis=1, keepdims=True)
        densities = jnp.where(lane == step, density, densities)
        if 0 < step <= count:
            kind = column_of(kinds, place, row)
            at = slice(step - 1, step)
            tails = [[source[count + 3, at, TILE * side:TILE * (side + 1)] for source in sources] for side in range(2) if carried]
            known = [(column_of(tail[0], lane[:1], 1), column_of(sum(tail), lane[:1], 0)) for tail in tails]
            for flip, (value, source) in enumerate(zip(values, sources)):
                for i in range(per):
                    at = lax.bitwise_xor(rank, flip) * per + i
                    table = tables_ref[at]
                    for tile, cell, out_ref in ((0, 0, first_ref), (1, cols - 1, last_ref)):
                        of = slice(TILE * tile, TILE * (tile + 1))
                        if carried:
                            raw = source[count + 2, step - 1:step, half * (1 - tile) + TILE * i:half * (1 - tile) + TILE * (i + 1)]
                            out_ref[(step - 1) * N + at] = walled(*known[1 - tile], raw, table, of)
                        else:
                            edge = walled(kind, density, value[:, PLANE * i + TILE * tile:PLANE * i + TILE * (tile + 1)], table, of)
                            out_ref[(step - 1) * N + at] = edge[cell:cell + 1]
    density_ref[...] = densities


def collide_body(groups, dirs, batch, first_row, rank_ref, *refs):
    sources, refs = refs[:groups], refs[groups:]
    before_ref, after_ref, density_ref, kind_ref, tables_ref, low_ref, top_ref, matrix_ref, _ = refs[:9]
    outs, refs = refs[9:9 + groups], refs[9 + groups:]
    moved_refs, spec_refs, gain_ref = refs[:2], refs[2:4], refs[4]
    given, kept, sems = (matrix_ref, low_ref, top_ref), refs[5:8], refs[8]
    copies = [pltpu.make_async_copy(value, into, sems.at[at]) for at, (value, into) in enumerate(zip(given, kept))]
    matrix_ref, low_ref, top_ref = kept
    for copy in copies:
        copy.start()
    copies[0].wait()
    rows = N * CELLS
    per = N // groups
    steps = outs[0].shape[0]
    total_rows = kind_ref.shape[1]
    own_rows = total_rows // groups
    rank = rank_ref[0]
    sub = lax.broadcasted_iota(jnp.int32, (CELLS, TILE), 0)
    place = lax.broadcasted_iota(jnp.int32, kind_ref.shape, 1)
    lane = lax.broadcasted_iota(jnp.int32, density_ref.shape, 1)
    kinds, densities = kind_ref[...], density_ref[...]
    origin = rank * own_rows + first_row
    start = window(rank, own_rows, total_rows, first_row, steps)

    def cells_of(step):
        row = jnp.clip(origin + step, 0, total_rows - 1)
        return row - start, column_of(kinds, place, row), column_of(densities, lane, step + 1)

    def turned(value, at):
        straight, crossed = dot(value, matrix_ref[at]), dot(value, matrix_ref[at + 1])
        return jnp.concatenate([straight[:rows] + crossed[rows:], straight[rows:] - crossed[:rows]], 0)

    def prepare(step, moved_ref, spec_ref):
        now_at, kind, density = cells_of(step)
        past, ahead = cells_of(step - 1), cells_of(step + 1)
        for flip, source in enumerate(sources):
            owner = lax.bitwise_xor(rank, flip)
            positive = owner >= groups // 2
            other_at, other_kind, other_density = (jnp.where(positive, p, a) for p, a in zip(past, ahead))
            for i in range(per):
                line = owner * per + i
                table = tables_ref[line]
                for tile in range(2):
                    at = slice(TILE * tile, TILE * (tile + 1))
                    of = slice(PLANE * i + TILE * tile, PLANE * i + TILE * (tile + 1))
                    now = walled(kind, density, source[now_at, :, of], table, at)
                    other = walled(other_kind, other_density, source[other_at, :, of], table, at)
                    if tile:
                        near = jnp.where(sub == 0, before_ref[step * N + line], pltpu.roll(now, 1, 0))
                    else:
                        near = jnp.where(sub == CELLS - 1, after_ref[step * N + line], pltpu.roll(now, CELLS - 1, 0))
                    drift = table[0:1, at] * (now - other) + table[1:2, at] * (now - near)
                    moved_ref[line, :, at] = jnp.where(kind == 0.0, now - courant * drift, now)
        yield
        value = dot(matrix_ref[0, :, :rows], moved_ref[...].reshape(rows, PLANE).astype(bf16)).astype(bf16)
        yield
        value = turned(value, 1).astype(bf16)
        yield
        spec_ref[...] = turned(value, 3).astype(bf16).astype(f32)
        yield

    def finish(step, moved_ref, spec_ref, beside):
        def weighted(*pair):
            parts = [[] for _ in pair]
            for i in range(N):
                re_at, im_at = slice(CELLS * i, CELLS * (i + 1)), slice(rows + CELLS * i, rows + CELLS * (i + 1))
                low_re, top_re = spec_ref[re_at, :TILE], spec_ref[re_at, TILE:]
                low_im, top_im = spec_ref[im_at, :TILE], spec_ref[im_at, TILE:]
                for p, part in zip(pair, parts):
                    low, top = low_ref[i, p:p + 1, :], top_ref[i, p:p + 1, :]
                    part.append(low * low_re - top * top_im)
                    part.append(low * low_im + top * top_re)
            return jnp.concatenate([jnp.concatenate(part, 0) for part in parts], 1).astype(bf16)

        def along_i(*pair):
            value = dot(matrix_ref[5], weighted(*pair)).astype(bf16)
            return [jnp.concatenate([value[:rows, TILE * t:TILE * (t + 1)], value[rows:, TILE * t:TILE * (t + 1)]], 1)
                    for t in range(len(pair))]

        gain_ref[...] = jnp.zeros_like(gain_ref)
        for first in range(0, dirs, batch):
            stack = []
            for p in range(first, min(first + batch, dirs)):
                stack += along_i(p, dirs + p)
            value = dot(jnp.concatenate(stack, 0), matrix_ref[6])
            total = gain_ref[...]
            for at in range(0, value.shape[0], 2 * rows):
                total = total + value[at:at + rows] * value[at + rows:at + 2 * rows]
            gain_ref[...] = total
            next(beside, None)
        for _ in beside:
            pass
        loss = dot(along_i(2 * dirs)[0], matrix_ref[6])
        now = moved_ref[...]
        collision = (gain_ref[...] - now.reshape(rows, PLANE) * loss).reshape(N, CELLS, PLANE)
        moved_ref[...] = jnp.where(cells_of(step)[1] == 0.0, now + collision_timestep * collision, now)
        for flip, out_ref in enumerate(outs):
            at = lax.bitwise_xor(rank, flip) * per
            for i in range(per):
                out_ref[step, :, PLANE * i:PLANE * (i + 1)] = moved_ref[at + i]

    for _ in prepare(0, moved_refs[0], spec_refs[0]):
        pass
    copies[1].wait()
    copies[2].wait()

    def two_rows(pair, _):
        one, other = 2 * pair, jnp.minimum(2 * pair + 1, steps - 1)
        following = jnp.minimum(2 * pair + 2, steps - 1)
        finish(one, moved_refs[0], spec_refs[0], prepare(other, moved_refs[1], spec_refs[1]))
        finish(other, moved_refs[1], spec_refs[1], prepare(following, moved_refs[0], spec_refs[0]))
        return 0

    lax.fori_loop(0, (steps + 1) // 2, two_rows, 0)


def place_body(groups, starts, rank_ref, *refs):
    pieces, (out_ref, sems) = refs[:-2], refs[-2:]
    own_rows = out_ref.shape[0] // groups
    copies = []
    for at, piece in enumerate(pieces):
        top = lax.bitwise_xor(rank_ref[0], at % groups) * own_rows + starts[at // groups]
        copies.append(pltpu.make_async_copy(piece, out_ref.at[pl.ds(top, piece.shape[0])], sems.at[at]))
    for copy in copies:
        copy.start()
    for copy in copies:
        copy.wait()


def collide(rank, sources, before, after, density, kinds, tables, low, top, matrices, earlier, first_row, steps):
    groups = len(sources)
    dirs = low.shape[1] // 3
    _, cols, width = sources[0].shape
    vmem = pl.BlockSpec(memory_space=pltpu.VMEM)
    shape = jax.ShapeDtypeStruct((steps, cols, width), f32)
    operands = (*sources, before, after, density, kinds, tables, low, top, matrices, earlier)
    cells = pltpu.VMEM((N, CELLS, PLANE), f32)
    spec = pltpu.VMEM((2 * N * CELLS, PLANE), f32)
    return call(
        functools.partial(collide_body, groups, dirs, 4, first_row), (shape,) * groups, (rank, *operands),
        flops=steps * 2 * PLANE ** 3 * (2 * dirs + 6), limit=6,
        scratch=[cells, cells, spec, spec, pltpu.VMEM((N * CELLS, PLANE), f32)]
        + [pltpu.VMEM(value.shape, value.dtype) for value in (matrices, low, top)] + [pltpu.SemaphoreType.DMA((3,))],
        in_specs=[pl.BlockSpec(memory_space=pltpu.SMEM)] + [vmem] * (len(operands) - 1) + [pl.BlockSpec(memory_space=pl.ANY)],
        out_specs=(vmem,) * groups,
    )


def on_device(distribution, cell_type, first_kernel, second_kernel, loss_kernel):
    rows, cols, width = distribution.shape
    groups = lax.axis_size("vel")
    rank = lax.axis_index("vel")
    spots = lax.axis_size("cell")
    own_rows = rows // groups
    half = (own_rows // 4) * 2
    chunks = [(0, half), (half, own_rows - half)]
    rank_word = rank.astype(jnp.int32)[None]
    tables = jnp.asarray(velocity_tables())
    kinds = cell_type.astype(f32).T
    vmem = pl.BlockSpec(memory_space=pltpu.VMEM)
    smem = pl.BlockSpec(memory_space=pltpu.SMEM)
    anywhere = pl.BlockSpec(memory_space=pl.ANY)

    def swap(values):
        swapped = {0: values[0]}
        for flip in reversed(range(1, groups)):
            swapped[flip] = lax.ppermute(values[flip], "vel", [(i, i ^ flip) for i in range(groups)])
        return [swapped[flip] for flip in range(groups)]

    def cut(first_row, count, earlier, *columns):
        block = jax.ShapeDtypeStruct((count + 2 + len(columns), cols, width), f32)
        return call(
            functools.partial(cut_body, groups, first_row), (block,) * groups, (rank_word, distribution, earlier, *columns),
            in_specs=[smem, anywhere, anywhere] + [vmem] * len(columns), out_specs=(vmem,) * groups,
            scratch=[pltpu.SemaphoreType.DMA((groups,))])

    def rims(first_row, count, sources, *passing):
        edge = jax.ShapeDtypeStruct((count * N, 1, TILE), f32)
        same = [jax.ShapeDtypeStruct(value.shape, f32) for value in passing]
        return call(
            functools.partial(edges_body, groups, first_row, len(passing)),
            (edge, edge, jax.ShapeDtypeStruct((cols, TILE), f32), *same),
            (rank_word, *sources, matrices, kinds, tables, *passing),
            in_specs=[smem] + [vmem] * groups + [anywhere, vmem, vmem] + [anywhere] * len(passing),
            out_specs=(vmem,) * 3 + (anywhere,) * len(passing),
            input_output_aliases={groups + 4 + at: 3 + at for at in range(len(passing))})

    def to_neighbours(first, last):
        return (lax.ppermute(last, "cell", [(i, i + 1) for i in range(spots - 1)]),
                lax.ppermute(first, "cell", [(i + 1, i) for i in range(spots - 1)]))

    (first_row, count), (next_row, next_count) = chunks
    cuts = [lax.dynamic_slice_in_dim(distribution, window(rank ^ flip, own_rows, rows, first_row, count), count + 2, 0)
            for flip in range(groups)]
    sources = swap(cuts)
    low, top, matrices = setup(first_kernel, second_kernel, loss_kernel)
    column = jax.ShapeDtypeStruct((rows, 1, width // 2 + TILE), f32)
    columns = to_neighbours(*call(
        columns_body, (column, column), (distribution, kinds, cuts[0]), in_specs=[vmem, vmem, anywhere], out_specs=(vmem,) * 2))
    first, last, density = rims(first_row, count, sources)
    edges = to_neighbours(first, last)
    following = cut(next_row, next_count, density, *columns)
    done = collide(rank_word, sources, *edges, density, kinds, tables, low, top, matrices, following[0], first_row, count)
    sources = swap(following)
    after, before, density, *done = rims(next_row, next_count, sources, *done)
    home = swap(done)
    done = collide(rank_word, sources, before, after, density, kinds, tables, low, top, matrices, done[0], next_row, next_count)
    pieces = (*home, *swap(done))
    return call(
        functools.partial(place_body, groups, (first_row, next_row)), jax.ShapeDtypeStruct(distribution.shape, f32),
        (rank_word, *pieces), in_specs=[smem] + [vmem] * len(pieces), out_specs=anywhere,
        scratch=[pltpu.SemaphoreType.DMA((len(pieces),))])


def solution(mesh):
    return jax.shard_map(
        on_device,
        mesh=mesh,
        in_specs=(P(None, "cell", "vel"), P(None, "cell"), P(), P(), P()),
        out_specs=P(None, "cell", "vel"),
        check_vma=False,
    )
```

```python
import functools
import math

import jax
import jax.numpy as jnp
import numpy as np
from jax import lax
from jax.experimental import pallas as pl
from jax.experimental.pallas import tpu as pltpu
from jax.sharding import PartitionSpec as P

N = 16
HALF = N // 2
PLANE = N * N
TILE = N * HALF
CELLS = 8
courant = 0.45
collision_timestep = 0.1
bf16 = jnp.bfloat16
f32 = jnp.float32


def velocity_tables():
    levels = ((2.0 * np.arange(N, dtype=np.float32) - (N - 1)) / (N - 1)).astype(np.float64)
    cx = np.repeat(levels, PLANE)
    cy = np.tile(np.repeat(levels, N), N)
    cz = np.tile(levels, PLANE)
    still = np.exp(-4.5 * (cx * cx + cy * cy + cz * cz))
    moving = np.exp(-0.5 * ((3.0 * cx - 1.0) ** 2 + 9.0 * cy * cy + 9.0 * cz * cz))
    rows = [np.abs(cx), np.abs(cy), still / still.sum(), moving / moving.sum()]
    rows += [np.zeros_like(cx)] * (8 - len(rows))
    return np.stack(rows).astype(np.float32).reshape(8, N, PLANE).transpose(1, 0, 2)


def fourier_matrices():
    n = np.arange(N)
    angles = 2.0 * math.pi * ((n[:, None] * n[None, :]) % N) / N
    rounded = lambda t: t.astype(np.float32).astype(jnp.bfloat16).astype(np.float64)
    c, s = rounded(np.cos(angles)), rounded(np.sin(angles))
    by_cell, by_line = np.eye(CELLS), np.eye(N)
    forward_i = np.concatenate([np.kron(c, by_cell), np.kron(-s, by_cell)], 0)
    cj, sj = np.kron(c, by_line), np.kron(s, by_line)
    pick = half_selection()[:, :PLANE]
    ck, sk = np.kron(by_line, c) @ pick, np.kron(by_line, s) @ pick
    turn = np.stack([np.stack([c, -s], -1), np.stack([s, c], -1)], 0) / N
    inverse_i = np.kron(turn.reshape(2 * N, 2 * N), by_cell)
    c, s = c / N, s / N
    spread = lambda left, right: np.einsum("bj,d->jbd", left, right)
    last = np.zeros((2, N, HALF, N, N))
    for k in range(1, HALF):
        last[0, :, k] = 2.0 * (spread(c, c[:, k]) - spread(s, s[:, k]))
        last[1, :, k] = -2.0 * (spread(c, s[:, k]) + spread(s, c[:, k]))
    last[0, :, 0] = spread(c, c[:, 0]) + spread(s, c[:, HALF])
    last[1, :, 0] = spread(c, c[:, HALF]) - spread(s, c[:, 0])
    inverse_jk = last.reshape(PLANE, PLANE)
    forward_i = np.concatenate([forward_i, np.zeros_like(forward_i)], 1)
    return np.stack([forward_i, cj, sj, ck, sk, inverse_i, inverse_jk]).astype(np.float32)


def half_selection():
    eye = np.eye(PLANE, dtype=np.float32).reshape(PLANE, N, N)
    low = eye[..., :HALF]
    top = np.zeros_like(low)
    top[..., 0] = eye[..., HALF]
    straight = np.concatenate([low.reshape(PLANE, TILE), top.reshape(PLANE, TILE)], 1)
    flip = (-np.arange(N)) % N
    mirrored = straight.reshape(N, N, PLANE)[flip][:, flip].reshape(PLANE, PLANE)
    return np.concatenate([straight, mirrored], 1)


def dot(left, right):
    return jnp.dot(left, right, preferred_element_type=f32)


def call(kernel, out_shape, operands, flops=0, scratch=(), limit=2, **options):
    moved = sum(a.size * a.dtype.itemsize for a in list(operands) + jax.tree.leaves(out_shape))
    return pl.pallas_call(
        kernel, out_shape=out_shape, scratch_shapes=list(scratch),
        compiler_params=pltpu.CompilerParams(vmem_limit_bytes=limit * 2 ** 20),
        cost_estimate=pl.CostEstimate(flops=flops, bytes_accessed=moved, transcendentals=0),
        **options,
    )(*operands)


def setup_body(first_ref, second_ref, loss_ref, pick_ref, table_ref, low_ref, top_ref, matrix_ref):
    dirs = first_ref.shape[0]
    matrix_ref[...] = table_ref[...].astype(bf16)
    parts = []
    for i in range(N):
        at = slice(PLANE * i, PLANE * (i + 1))
        value = jnp.concatenate([first_ref[:, at], second_ref[:, at], jnp.broadcast_to(loss_ref[:, at], (dirs, PLANE))], 0)
        for _ in range(3):
            part = value.astype(bf16)
            value = value - part.astype(f32)
            parts.append(part)
    picked = dot(jnp.concatenate(parts, 0), pick_ref[...].astype(bf16)).reshape(N, 3, 3 * dirs, 2 * PLANE)
    picked = picked[:, 0] + picked[:, 1] + picked[:, 2]
    for i in range(N):
        even = 0.5 * (picked[i, :, :PLANE] + picked[-i % N, :, PLANE:])
        low_ref[i] = even[:, :TILE]
        top_ref[i] = even[:, TILE:]


def setup(first_kernel, second_kernel, loss_kernel):
    total = 3 * first_kernel.shape[0]
    shape = jax.ShapeDtypeStruct((N, total, TILE), f32)
    matrices = fourier_matrices()
    operands = (first_kernel, second_kernel, loss_kernel[None, :], jnp.asarray(half_selection()), jnp.asarray(matrices))
    return call(setup_body, (shape, shape, jax.ShapeDtypeStruct(matrices.shape, bf16)), operands,
                flops=6 * total * N * PLANE * 2 * PLANE)


def column_of(table, lane, row):
    return jnp.sum(jnp.where(lane == row, table, 0.0), axis=1, keepdims=True)


def walled(kind, density, raw, table, at):
    return jnp.where(kind == 0.0, raw, jnp.where(kind == 1.0, table[2:3, at], table[3:4, at]) * density)


def window(rank, own_rows, total_rows, first_row, count):
    return jnp.clip(rank * own_rows + first_row - 1, 0, total_rows - count - 2)


def columns_body(cells_ref, kind_ref, after_ref, first_ref, last_ref):
    del after_ref
    rows, cols, width = cells_ref.shape
    half = width // 2
    lane = lax.broadcasted_iota(jnp.int32, (cols, TILE), 1)
    place = lax.broadcasted_iota(jnp.int32, (cols, rows), 1)
    kinds = kind_ref[...]

    def one_row(row, _):
        values = cells_ref[row]
        total = jnp.sum(values, axis=1, keepdims=True)
        tail = jnp.where(lane == 0, total, jnp.where(lane == 1, column_of(kinds, place, row), 0.0))
        for block in range(width // PLANE):
            to = slice(TILE * block, TILE * (block + 1))
            at = PLANE * block
            first_ref[row, :, to] = values[:1, at:at + TILE]
            last_ref[row, :, to] = values[cols - 1:, at + TILE:at + PLANE]
        first_ref[row, :, half:] = tail[:1]
        last_ref[row, :, half:] = tail[cols - 1:]
        return 0

    lax.fori_loop(0, rows, one_row, 0, unroll=8)


def later_window(taker, own_rows, total_rows, first_row, count):
    return jnp.clip(taker * own_rows + first_row + 1, 0, total_rows - count)


def cut_body(groups, first_row, count, rank_ref, cells_ref, after_ref, *refs):
    del after_ref
    columns, outs, sems = refs[:-1 - groups], refs[-1 - groups:-1], refs[-1]
    rows = cells_ref.shape[0]
    own_rows = rows // groups
    copies = []
    for flip, out_ref in enumerate(outs):
        top = later_window(lax.bitwise_xor(rank_ref[0], flip), own_rows, rows, first_row, count)
        copies.append(pltpu.make_async_copy(cells_ref.at[pl.ds(top, count)], out_ref.at[pl.ds(0, count)], sems.at[flip]))
    for copy in copies:
        copy.start()
    for flip, out_ref in enumerate(outs):
        top = lax.bitwise_xor(rank_ref[0], flip) * own_rows + first_row
        for side, column in enumerate(columns):
            half = column.shape[2] - TILE
            for step in range(count):
                out_ref[count, step:step + 1, half * side:half * (side + 1)] = column[top + step, :, :half]
                out_ref[count + 1, step:step + 1, TILE * side:TILE * (side + 1)] = column[top + step, :, half:]
    for copy in copies:
        copy.wait()


def reader(sources, carried, rank, own_rows, total_rows, first_row, count):
    if not carried:
        start = window(rank, own_rows, total_rows, first_row, count)
        return lambda flip, row, of: sources[flip][row - start, :, of]
    origin = rank * own_rows + first_row
    start = later_window(rank, own_rows, total_rows, first_row, count)

    def read(flip, row, of):
        old = carried[flip][jnp.clip(row - origin + 1, 0, 1), :, of]
        new = sources[flip][jnp.clip(row - start, 0, count - 1), :, of]
        return jnp.where(row > origin, new, old)
    return read


def edges_body(groups, first_row, count, passing, later, rank_ref, *refs):
    sources, refs = refs[:groups], refs[groups:]
    carried, refs = (refs[:groups], refs[groups:]) if later else ((), refs)
    kind_ref, tables_ref = refs[1:3]
    first_ref, last_ref, density_ref = refs[3 + passing:6 + passing]
    keeps = () if later else refs[6 + passing:]
    cols, total_rows = kind_ref.shape
    half = sources[0].shape[2] // 2
    per = N // groups
    rank = rank_ref[0]
    own_rows = total_rows // groups
    kinds = kind_ref[...]
    place = lax.broadcasted_iota(jnp.int32, kinds.shape, 1)
    lane = lax.broadcasted_iota(jnp.int32, density_ref.shape, 1)
    read = reader(sources, carried, rank, own_rows, total_rows, first_row, count)
    for flip, keep in enumerate(keeps):
        for at in range(2):
            keep[at] = read(flip, rank * own_rows + first_row + count - 1 + at, slice(None))
    densities = jnp.zeros(density_ref.shape, f32)
    for step in range(count + 2):
        row = jnp.clip(rank * own_rows + first_row - 1 + step, 0, total_rows - 1)
        values = [read(flip, row, slice(None)) for flip in range(groups)]
        density = jnp.sum(sum(values), axis=1, keepdims=True)
        densities = jnp.where(lane == step, density, densities)
        if 0 < step <= count:
            kind = column_of(kinds, place, row)
            at = slice(step - 1, step)
            tails = [[source[count + 1, at, TILE * side:TILE * (side + 1)] for source in sources] for side in range(2) if later]
            known = [(column_of(tail[0], lane[:1], 1), column_of(sum(tail), lane[:1], 0)) for tail in tails]
            for flip, (value, source) in enumerate(zip(values, sources)):
                for i in range(per):
                    at = lax.bitwise_xor(rank, flip) * per + i
                    table = tables_ref[at]
                    for tile, cell, out_ref in ((0, 0, first_ref), (1, cols - 1, last_ref)):
                        of = slice(TILE * tile, TILE * (tile + 1))
                        if later:
                            raw = source[count, step - 1:step, half * (1 - tile) + TILE * i:half * (1 - tile) + TILE * (i + 1)]
                            out_ref[(step - 1) * N + at] = walled(*known[1 - tile], raw, table, of)
                        else:
                            edge = walled(kind, density, value[:, PLANE * i + TILE * tile:PLANE * i + TILE * (tile + 1)], table, of)
                            out_ref[(step - 1) * N + at] = edge[cell:cell + 1]
    density_ref[...] = densities


def collide_body(groups, dirs, batch, first_row, later, rank_ref, *refs):
    sources, refs = refs[:groups], refs[groups:]
    carried, refs = (refs[:groups], refs[groups:]) if later else ((), refs)
    before_ref, after_ref, density_ref, kind_ref, tables_ref, low_ref, top_ref, matrix_ref, _ = refs[:9]
    outs, refs = refs[9:9 + groups], refs[9 + groups:]
    moved_refs, spec_refs, gain_ref = refs[:2], refs[2:4], refs[4]
    given, kept, sems = (matrix_ref, low_ref, top_ref), refs[5:8], refs[8]
    copies = [pltpu.make_async_copy(value, into, sems.at[at]) for at, (value, into) in enumerate(zip(given, kept))]
    matrix_ref, low_ref, top_ref = kept
    for copy in copies:
        copy.start()
    rows = N * CELLS
    per = N // groups
    steps = outs[0].shape[0]
    total_rows = kind_ref.shape[1]
    own_rows = total_rows // groups
    rank = rank_ref[0]
    sub = lax.broadcasted_iota(jnp.int32, (CELLS, TILE), 0)
    place = lax.broadcasted_iota(jnp.int32, kind_ref.shape, 1)
    lane = lax.broadcasted_iota(jnp.int32, density_ref.shape, 1)
    kinds, densities = kind_ref[...], density_ref[...]
    origin = rank * own_rows + first_row
    read = reader(sources, carried, rank, own_rows, total_rows, first_row, steps)

    def cells_of(step):
        row = jnp.clip(origin + step, 0, total_rows - 1)
        return row, column_of(kinds, place, row), column_of(densities, lane, step + 1)

    def turned(value, at):
        straight, crossed = dot(value, matrix_ref[at]), dot(value, matrix_ref[at + 1])
        return jnp.concatenate([straight[:rows] + crossed[rows:], straight[rows:] - crossed[:rows]], 0)

    def prepare(step, moved_ref, spec_ref):
        now_at, kind, density = cells_of(step)
        past, ahead = cells_of(step - 1), cells_of(step + 1)
        for flip, source in enumerate(sources):
            owner = lax.bitwise_xor(rank, flip)
            positive = owner >= groups // 2
            other_at, other_kind, other_density = (jnp.where(positive, p, a) for p, a in zip(past, ahead))
            for i in range(per):
                line = owner * per + i
                table = tables_ref[line]
                for tile in range(2):
                    at = slice(TILE * tile, TILE * (tile + 1))
                    of = slice(PLANE * i + TILE * tile, PLANE * i + TILE * (tile + 1))
                    now = walled(kind, density, read(flip, now_at, of), table, at)
                    other = walled(other_kind, other_density, read(flip, other_at, of), table, at)
                    if tile:
                        near = jnp.where(sub == 0, before_ref[step * N + line], pltpu.roll(now, 1, 0))
                    else:
                        near = jnp.where(sub == CELLS - 1, after_ref[step * N + line], pltpu.roll(now, CELLS - 1, 0))
                    drift = table[0:1, at] * (now - other) + table[1:2, at] * (now - near)
                    moved_ref[line, :, at] = jnp.where(kind == 0.0, now - courant * drift, now)
        yield
        value = dot(matrix_ref[0, :, :rows], moved_ref[...].reshape(rows, PLANE).astype(bf16)).astype(bf16)
        yield
        value = turned(value, 1).astype(bf16)
        yield
        spec_ref[...] = turned(value, 3).astype(bf16).astype(f32)
        yield

    def finish(step, moved_ref, spec_ref, beside):
        def weighted(*pair):
            parts = [[] for _ in pair]
            for i in range(N):
                re_at, im_at = slice(CELLS * i, CELLS * (i + 1)), slice(rows + CELLS * i, rows + CELLS * (i + 1))
                low_re, top_re = spec_ref[re_at, :TILE], spec_ref[re_at, TILE:]
                low_im, top_im = spec_ref[im_at, :TILE], spec_ref[im_at, TILE:]
                for p, part in zip(pair, parts):
                    low, top = low_ref[i, p:p + 1, :], top_ref[i, p:p + 1, :]
                    part.append(low * low_re - top * top_im)
                    part.append(low * low_im + top * top_re)
            return jnp.concatenate([jnp.concatenate(part, 0) for part in parts], 1).astype(bf16)

        def along_i(*pair):
            value = dot(matrix_ref[5], weighted(*pair)).astype(bf16)
            return [jnp.concatenate([value[:rows, TILE * t:TILE * (t + 1)], value[rows:, TILE * t:TILE * (t + 1)]], 1)
                    for t in range(len(pair))]

        gain_ref[...] = jnp.zeros_like(gain_ref)
        for first in range(0, dirs, batch):
            stack = []
            for p in range(first, min(first + batch, dirs)):
                stack += along_i(p, dirs + p)
            value = dot(jnp.concatenate(stack, 0), matrix_ref[6])
            total = gain_ref[...]
            for at in range(0, value.shape[0], 2 * rows):
                total = total + value[at:at + rows] * value[at + rows:at + 2 * rows]
            gain_ref[...] = total
            next(beside, None)
        for _ in beside:
            pass
        loss = dot(along_i(2 * dirs)[0], matrix_ref[6])
        now = moved_ref[...]
        collision = (gain_ref[...] - now.reshape(rows, PLANE) * loss).reshape(N, CELLS, PLANE)
        moved_ref[...] = jnp.where(cells_of(step)[1] == 0.0, now + collision_timestep * collision, now)
        for flip, out_ref in enumerate(outs):
            at = lax.bitwise_xor(rank, flip) * per
            for i in range(per):
                out_ref[step, :, PLANE * i:PLANE * (i + 1)] = moved_ref[at + i]

    opening = prepare(0, moved_refs[0], spec_refs[0])
    next(opening)
    copies[0].wait()
    for _ in opening:
        pass
    copies[1].wait()
    copies[2].wait()

    def two_rows(pair, _):
        finish(2 * pair, moved_refs[0], spec_refs[0], prepare(2 * pair + 1, moved_refs[1], spec_refs[1]))
        finish(2 * pair + 1, moved_refs[1], spec_refs[1], prepare(2 * pair + 2, moved_refs[0], spec_refs[0]))
        return 0

    lax.fori_loop(0, (steps - 1) // 2, two_rows, 0)
    if steps % 2 == 0:
        finish(steps - 2, moved_refs[0], spec_refs[0], prepare(steps - 1, moved_refs[1], spec_refs[1]))
    last = (steps - 1) % 2
    finish(steps - 1, moved_refs[last], spec_refs[last], iter(()))


def place_body(groups, places, rank_ref, *refs):
    pieces, refs = refs[:len(places)], refs[len(places):]
    out_ref, sems = refs[-2:]
    own_rows = out_ref.shape[0] // groups
    copies = []
    for at, (piece, (flip, first_row)) in enumerate(zip(pieces, places)):
        top = lax.bitwise_xor(rank_ref[0], flip) * own_rows + first_row
        copies.append(pltpu.make_async_copy(piece, out_ref.at[pl.ds(top, piece.shape[0])], sems.at[at]))
    for copy in copies:
        copy.start()
    for copy in copies:
        copy.wait()


def collide(rank, sources, carried, before, after, density, kinds, tables, low, top, matrices, earlier, first_row, steps):
    groups = len(sources)
    dirs = low.shape[1] // 3
    _, cols, width = sources[0].shape
    vmem = pl.BlockSpec(memory_space=pltpu.VMEM)
    shape = jax.ShapeDtypeStruct((steps, cols, width), f32)
    operands = (*sources, *carried, before, after, density, kinds, tables, low, top, matrices, earlier)
    cells = pltpu.VMEM((N, CELLS, PLANE), f32)
    spec = pltpu.VMEM((2 * N * CELLS, PLANE), f32)
    return call(
        functools.partial(collide_body, groups, dirs, 4, first_row, bool(carried)), (shape,) * groups, (rank, *operands),
        flops=steps * 2 * PLANE ** 3 * (2 * dirs + 6), limit=6,
        scratch=[cells, cells, spec, spec, pltpu.VMEM((N * CELLS, PLANE), f32)]
        + [pltpu.VMEM(value.shape, value.dtype) for value in (matrices, low, top)] + [pltpu.SemaphoreType.DMA((3,))],
        in_specs=[pl.BlockSpec(memory_space=pltpu.SMEM)] + [vmem] * (len(operands) - 1) + [pl.BlockSpec(memory_space=pl.ANY)],
        out_specs=(vmem,) * groups,
    )


def on_device(distribution, cell_type, first_kernel, second_kernel, loss_kernel):
    rows, cols, width = distribution.shape
    groups = lax.axis_size("vel")
    rank = lax.axis_index("vel")
    spots = lax.axis_size("cell")
    own_rows = rows // groups
    half = (own_rows // 4) * 2
    chunks = [(0, half), (half, own_rows - half)]
    rank_word = rank.astype(jnp.int32)[None]
    tables = jnp.asarray(velocity_tables())
    kinds = cell_type.astype(f32).T
    vmem = pl.BlockSpec(memory_space=pltpu.VMEM)
    smem = pl.BlockSpec(memory_space=pltpu.SMEM)
    anywhere = pl.BlockSpec(memory_space=pl.ANY)

    def swap(values):
        swapped = {0: values[0]}
        for flip in reversed(range(1, groups)):
            swapped[flip] = lax.ppermute(values[flip], "vel", [(i, i ^ flip) for i in range(groups)])
        return [swapped[flip] for flip in range(groups)]

    def cut(first_row, count, earlier, *columns):
        block = jax.ShapeDtypeStruct((count + 2, cols, width), f32)
        return call(
            functools.partial(cut_body, groups, first_row, count), (block,) * groups, (rank_word, distribution, earlier, *columns),
            in_specs=[smem, anywhere, anywhere] + [vmem] * len(columns), out_specs=(vmem,) * groups,
            scratch=[pltpu.SemaphoreType.DMA((groups,))])

    def rims(first_row, count, sources, carried=(), passing=()):
        edge = jax.ShapeDtypeStruct((count * N, 1, TILE), f32)
        same = [jax.ShapeDtypeStruct(value.shape, f32) for value in passing]
        keep = [] if carried else [jax.ShapeDtypeStruct((2, cols, width), f32)] * groups
        before = 1 + len(sources) + len(carried) + 3
        return call(
            functools.partial(edges_body, groups, first_row, count, len(passing), bool(carried)),
            (edge, edge, jax.ShapeDtypeStruct((cols, TILE), f32), *same, *keep),
            (rank_word, *sources, *carried, matrices, kinds, tables, *passing),
            in_specs=[smem] + [vmem] * (before - 4) + [anywhere, vmem, vmem] + [anywhere] * len(passing),
            out_specs=(vmem,) * 3 + (anywhere,) * len(passing) + (vmem,) * len(keep),
            input_output_aliases={before + at: 3 + at for at in range(len(passing))})

    def to_neighbours(first, last):
        return (lax.ppermute(last, "cell", [(i, i + 1) for i in range(spots - 1)]),
                lax.ppermute(first, "cell", [(i + 1, i) for i in range(spots - 1)]))

    (first_row, count), (next_row, next_count) = chunks
    cuts = [lax.dynamic_slice_in_dim(distribution, window(rank ^ flip, own_rows, rows, first_row, count), count + 2, 0)
            for flip in range(groups)]
    sources = swap(cuts)
    low, top, matrices = setup(first_kernel, second_kernel, loss_kernel)
    column = jax.ShapeDtypeStruct((rows, 1, width // 2 + TILE), f32)
    columns = to_neighbours(*call(
        columns_body, (column, column), (distribution, kinds, cuts[0]), in_specs=[vmem, vmem, anywhere], out_specs=(vmem,) * 2))
    first, last, density, *carried = rims(first_row, count, sources)
    edges = to_neighbours(first, last)
    following = cut(next_row, next_count, density, *columns)
    done = collide(rank_word, sources, (), *edges, density, kinds, tables, low, top, matrices, following[0], first_row, count)
    sources = swap(following)
    after, before, density, *done = rims(next_row, next_count, sources, carried, done)
    home = swap(done)
    done = collide(rank_word, sources, carried, before, after, density, kinds, tables, low, top, matrices, done[0], next_row, next_count)
    pieces = (*home, *swap(done))
    places = [(flip, row) for row in (first_row, next_row) for flip in range(groups)]
    return call(
        functools.partial(place_body, groups, places), jax.ShapeDtypeStruct(distribution.shape, f32),
        (rank_word, *pieces), in_specs=[smem] + [vmem] * len(pieces), out_specs=anywhere,
        scratch=[pltpu.SemaphoreType.DMA((len(pieces),))])


def solution(mesh):
    return jax.shard_map(
        on_device,
        mesh=mesh,
        in_specs=(P(None, "cell", "vel"), P(None, "cell"), P(), P(), P()),
        out_specs=P(None, "cell", "vel"),
        check_vma=False,
    )
```

```python
import functools
import math

import jax
import jax.numpy as jnp
import numpy as np
from jax import lax
from jax.experimental import pallas as pl
from jax.experimental.pallas import tpu as pltpu
from jax.sharding import PartitionSpec as P

N = 16
HALF = N // 2
PLANE = N * N
TILE = N * HALF
CELLS = 8
courant = 0.45
collision_timestep = 0.1
bf16 = jnp.bfloat16
f32 = jnp.float32


def velocity_tables():
    levels = ((2.0 * np.arange(N, dtype=np.float32) - (N - 1)) / (N - 1)).astype(np.float64)
    cx = np.repeat(levels, PLANE)
    cy = np.tile(np.repeat(levels, N), N)
    cz = np.tile(levels, PLANE)
    still = np.exp(-4.5 * (cx * cx + cy * cy + cz * cz))
    moving = np.exp(-0.5 * ((3.0 * cx - 1.0) ** 2 + 9.0 * cy * cy + 9.0 * cz * cz))
    rows = [np.abs(cx), np.abs(cy), still / still.sum(), moving / moving.sum()]
    rows += [np.zeros_like(cx)] * (8 - len(rows))
    return np.stack(rows).astype(np.float32).reshape(8, N, PLANE).transpose(1, 0, 2)


def fourier_matrices():
    n = np.arange(N)
    angles = 2.0 * math.pi * ((n[:, None] * n[None, :]) % N) / N
    rounded = lambda t: t.astype(np.float32).astype(jnp.bfloat16).astype(np.float64)
    c, s = rounded(np.cos(angles)), rounded(np.sin(angles))
    by_cell, by_line = np.eye(CELLS), np.eye(N)
    forward_i = np.concatenate([np.kron(c, by_cell), np.kron(-s, by_cell)], 0)
    cj, sj = np.kron(c, by_line), np.kron(s, by_line)
    pick = half_selection()[:, :PLANE]
    ck, sk = np.kron(by_line, c) @ pick, np.kron(by_line, s) @ pick
    turn = np.stack([np.stack([c, -s], -1), np.stack([s, c], -1)], 0) / N
    inverse_i = np.kron(turn.reshape(2 * N, 2 * N), by_cell)
    c, s = c / N, s / N
    spread = lambda left, right: np.einsum("bj,d->jbd", left, right)
    last = np.zeros((2, N, HALF, N, N))
    for k in range(1, HALF):
        last[0, :, k] = 2.0 * (spread(c, c[:, k]) - spread(s, s[:, k]))
        last[1, :, k] = -2.0 * (spread(c, s[:, k]) + spread(s, c[:, k]))
    last[0, :, 0] = spread(c, c[:, 0]) + spread(s, c[:, HALF])
    last[1, :, 0] = spread(c, c[:, HALF]) - spread(s, c[:, 0])
    inverse_jk = last.reshape(PLANE, PLANE)
    forward_i = np.concatenate([forward_i, np.zeros_like(forward_i)], 1)
    return np.stack([forward_i, cj, sj, ck, sk, inverse_i, inverse_jk]).astype(np.float32)


def half_selection():
    eye = np.eye(PLANE, dtype=np.float32).reshape(PLANE, N, N)
    low = eye[..., :HALF]
    top = np.zeros_like(low)
    top[..., 0] = eye[..., HALF]
    straight = np.concatenate([low.reshape(PLANE, TILE), top.reshape(PLANE, TILE)], 1)
    flip = (-np.arange(N)) % N
    mirrored = straight.reshape(N, N, PLANE)[flip][:, flip].reshape(PLANE, PLANE)
    return np.concatenate([straight, mirrored], 1)


def dot(left, right):
    return jnp.dot(left, right, preferred_element_type=f32)


def call(kernel, out_shape, operands, flops=0, scratch=(), limit=2, **options):
    moved = sum(a.size * a.dtype.itemsize for a in list(operands) + jax.tree.leaves(out_shape))
    return pl.pallas_call(
        kernel, out_shape=out_shape, scratch_shapes=list(scratch),
        compiler_params=pltpu.CompilerParams(vmem_limit_bytes=limit * 2 ** 20),
        cost_estimate=pl.CostEstimate(flops=flops, bytes_accessed=moved, transcendentals=0),
        **options,
    )(*operands)


def setup_body(first_ref, second_ref, loss_ref, pick_ref, table_ref, low_ref, top_ref, matrix_ref):
    dirs = first_ref.shape[0]
    matrix_ref[...] = table_ref[...].astype(bf16)
    parts = []
    for i in range(N):
        at = slice(PLANE * i, PLANE * (i + 1))
        value = jnp.concatenate([first_ref[:, at], second_ref[:, at], jnp.broadcast_to(loss_ref[:, at], (dirs, PLANE))], 0)
        for _ in range(3):
            part = value.astype(bf16)
            value = value - part.astype(f32)
            parts.append(part)
    picked = dot(jnp.concatenate(parts, 0), pick_ref[...].astype(bf16)).reshape(N, 3, 3 * dirs, 2 * PLANE)
    picked = picked[:, 0] + picked[:, 1] + picked[:, 2]
    for i in range(N):
        even = 0.5 * (picked[i, :, :PLANE] + picked[-i % N, :, PLANE:])
        low_ref[i] = even[:, :TILE]
        top_ref[i] = even[:, TILE:]


def setup(first_kernel, second_kernel, loss_kernel):
    total = 3 * first_kernel.shape[0]
    shape = jax.ShapeDtypeStruct((N, total, TILE), f32)
    matrices = fourier_matrices()
    operands = (first_kernel, second_kernel, loss_kernel[None, :], jnp.asarray(half_selection()), jnp.asarray(matrices))
    return call(setup_body, (shape, shape, jax.ShapeDtypeStruct(matrices.shape, bf16)), operands,
                flops=6 * total * N * PLANE * 2 * PLANE)


def column_of(table, lane, row):
    return jnp.sum(jnp.where(lane == row, table, 0.0), axis=1, keepdims=True)


def walled(kind, density, raw, table, at):
    return jnp.where(kind == 0.0, raw, jnp.where(kind == 1.0, table[2:3, at], table[3:4, at]) * density)


def window(rank, own_rows, total_rows, first_row, count):
    return jnp.clip(rank * own_rows + first_row - 1, 0, total_rows - count - 2)


def columns_body(cells_ref, kind_ref, after_ref, first_ref, last_ref):
    del after_ref
    rows, cols, width = cells_ref.shape
    half = width // 2
    lane = lax.broadcasted_iota(jnp.int32, (cols, TILE), 1)
    place = lax.broadcasted_iota(jnp.int32, (cols, rows), 1)
    kinds = kind_ref[...]

    def one_row(row, _):
        values = cells_ref[row]
        total = jnp.sum(values, axis=1, keepdims=True)
        tail = jnp.where(lane == 0, total, jnp.where(lane == 1, column_of(kinds, place, row), 0.0))
        for block in range(width // PLANE):
            to = slice(TILE * block, TILE * (block + 1))
            at = PLANE * block
            first_ref[row, :, to] = values[:1, at:at + TILE]
            last_ref[row, :, to] = values[cols - 1:, at + TILE:at + PLANE]
        first_ref[row, :, half:] = tail[:1]
        last_ref[row, :, half:] = tail[cols - 1:]
        return 0

    lax.fori_loop(0, rows, one_row, 0, unroll=8)


def later_window(taker, own_rows, total_rows, first_row, count):
    return jnp.clip(taker * own_rows + first_row + 1, 0, total_rows - count)


def cut_body(groups, first_row, count, rank_ref, cells_ref, after_ref, *refs):
    del after_ref
    columns, outs, sems = refs[:-1 - groups], refs[-1 - groups:-1], refs[-1]
    rows = cells_ref.shape[0]
    own_rows = rows // groups
    copies = []
    for flip, out_ref in enumerate(outs):
        top = later_window(lax.bitwise_xor(rank_ref[0], flip), own_rows, rows, first_row, count)
        copies.append(pltpu.make_async_copy(cells_ref.at[pl.ds(top, count)], out_ref.at[pl.ds(0, count)], sems.at[flip]))
    for copy in copies:
        copy.start()
    for flip, out_ref in enumerate(outs):
        top = lax.bitwise_xor(rank_ref[0], flip) * own_rows + first_row
        for side, column in enumerate(columns):
            half = column.shape[2] - TILE
            for step in range(count):
                out_ref[count, step:step + 1, half * side:half * (side + 1)] = column[top + step, :, :half]
                out_ref[count + 1, step:step + 1, TILE * side:TILE * (side + 1)] = column[top + step, :, half:]
    for copy in copies:
        copy.wait()


def reader(sources, carried, rank, own_rows, total_rows, first_row, count):
    if not carried:
        start = window(rank, own_rows, total_rows, first_row, count)
        return lambda flip, row, of: sources[flip][row - start, :, of]
    origin = rank * own_rows + first_row
    start = later_window(rank, own_rows, total_rows, first_row, count)

    def read(flip, row, of):
        old = carried[flip][jnp.clip(row - origin + 1, 0, 1), :, of]
        new = sources[flip][jnp.clip(row - start, 0, count - 1), :, of]
        return jnp.where(row > origin, new, old)
    return read


def edges_body(groups, first_row, count, passing, later, rank_ref, *refs):
    sources, refs = refs[:groups], refs[groups:]
    carried, refs = (refs[:groups], refs[groups:]) if later else ((), refs)
    kind_ref, tables_ref = refs[1:3]
    first_ref, last_ref, density_ref = refs[3 + passing:6 + passing]
    keeps = () if later else refs[6 + passing:]
    cols, total_rows = kind_ref.shape
    half = sources[0].shape[2] // 2
    per = N // groups
    rank = rank_ref[0]
    own_rows = total_rows // groups
    kinds = kind_ref[...]
    place = lax.broadcasted_iota(jnp.int32, kinds.shape, 1)
    lane = lax.broadcasted_iota(jnp.int32, density_ref.shape, 1)
    read = reader(sources, carried, rank, own_rows, total_rows, first_row, count)
    for flip, keep in enumerate(keeps):
        for at in range(2):
            keep[at] = read(flip, rank * own_rows + first_row + count - 1 + at, slice(None))
    densities = jnp.zeros(density_ref.shape, f32)
    for step in range(count + 2):
        row = jnp.clip(rank * own_rows + first_row - 1 + step, 0, total_rows - 1)
        values = [read(flip, row, slice(None)) for flip in range(groups)]
        density = jnp.sum(sum(values), axis=1, keepdims=True)
        densities = jnp.where(lane == step, density, densities)
        if 0 < step <= count:
            kind = column_of(kinds, place, row)
            at = slice(step - 1, step)
            tails = [[source[count + 1, at, TILE * side:TILE * (side + 1)] for source in sources] for side in range(2) if later]
            known = [(column_of(tail[0], lane[:1], 1), column_of(sum(tail), lane[:1], 0)) for tail in tails]
            for flip, (value, source) in enumerate(zip(values, sources)):
                for i in range(per):
                    at = lax.bitwise_xor(rank, flip) * per + i
                    table = tables_ref[at]
                    for tile, cell, out_ref in ((0, 0, first_ref), (1, cols - 1, last_ref)):
                        of = slice(TILE * tile, TILE * (tile + 1))
                        if later:
                            raw = source[count, step - 1:step, half * (1 - tile) + TILE * i:half * (1 - tile) + TILE * (i + 1)]
                            out_ref[(step - 1) * N + at] = walled(*known[1 - tile], raw, table, of)
                        else:
                            edge = walled(kind, density, value[:, PLANE * i + TILE * tile:PLANE * i + TILE * (tile + 1)], table, of)
                            out_ref[(step - 1) * N + at] = edge[cell:cell + 1]
    density_ref[...] = densities


def collide_body(groups, dirs, batch, first_row, later, rank_ref, *refs):
    sources, refs = refs[:groups], refs[groups:]
    carried, refs = (refs[:groups], refs[groups:]) if later else ((), refs)
    before_ref, after_ref, density_ref, kind_ref, tables_ref, low_ref, top_ref, matrix_ref, _ = refs[:9]
    outs, refs = refs[9:9 + groups], refs[9 + groups:]
    moved_refs, spec_refs, gain_ref = refs[:2], refs[2:4], refs[4]
    given, kept, sems = (matrix_ref, low_ref, top_ref), refs[5:8], refs[8]
    copies = [pltpu.make_async_copy(value, into, sems.at[at]) for at, (value, into) in enumerate(zip(given, kept))]
    matrix_ref, low_ref, top_ref = kept
    for copy in copies:
        copy.start()
    rows = N * CELLS
    per = N // groups
    steps = outs[0].shape[0]
    total_rows = kind_ref.shape[1]
    own_rows = total_rows // groups
    rank = rank_ref[0]
    sub = lax.broadcasted_iota(jnp.int32, (CELLS, TILE), 0)
    place = lax.broadcasted_iota(jnp.int32, kind_ref.shape, 1)
    lane = lax.broadcasted_iota(jnp.int32, density_ref.shape, 1)
    kinds, densities = kind_ref[...], density_ref[...]
    origin = rank * own_rows + first_row
    read = reader(sources, carried, rank, own_rows, total_rows, first_row, steps)

    def cells_of(step):
        row = jnp.clip(origin + step, 0, total_rows - 1)
        return row, column_of(kinds, place, row), column_of(densities, lane, step + 1)

    def turned(value, at):
        straight, crossed = dot(value, matrix_ref[at]), dot(value, matrix_ref[at + 1])
        return jnp.concatenate([straight[:rows] + crossed[rows:], straight[rows:] - crossed[:rows]], 0)

    def prepare(step, moved_ref, spec_ref):
        now_at, kind, density = cells_of(step)
        past, ahead = cells_of(step - 1), cells_of(step + 1)
        for flip, source in enumerate(sources):
            owner = lax.bitwise_xor(rank, flip)
            positive = owner >= groups // 2
            other_at, other_kind, other_density = (jnp.where(positive, p, a) for p, a in zip(past, ahead))
            for i in range(per):
                line = owner * per + i
                table = tables_ref[line]
                for tile in range(2):
                    at = slice(TILE * tile, TILE * (tile + 1))
                    of = slice(PLANE * i + TILE * tile, PLANE * i + TILE * (tile + 1))
                    now = walled(kind, density, read(flip, now_at, of), table, at)
                    other = walled(other_kind, other_density, read(flip, other_at, of), table, at)
                    if tile:
                        near = jnp.where(sub == 0, before_ref[step * N + line], pltpu.roll(now, 1, 0))
                    else:
                        near = jnp.where(sub == CELLS - 1, after_ref[step * N + line], pltpu.roll(now, CELLS - 1, 0))
                    drift = table[0:1, at] * (now - other) + table[1:2, at] * (now - near)
                    moved_ref[line, :, at] = jnp.where(kind == 0.0, now - courant * drift, now)
        yield
        value = dot(matrix_ref[0, :, :rows], moved_ref[...].reshape(rows, PLANE).astype(bf16)).astype(bf16)
        yield
        value = turned(value, 1).astype(bf16)
        yield
        spec_ref[...] = turned(value, 3).astype(bf16).astype(f32)
        yield

    def finish(step, moved_ref, spec_ref, beside):
        def weighted(*pair):
            parts = [[] for _ in pair]
            for i in range(N):
                re_at, im_at = slice(CELLS * i, CELLS * (i + 1)), slice(rows + CELLS * i, rows + CELLS * (i + 1))
                low_re, top_re = spec_ref[re_at, :TILE], spec_ref[re_at, TILE:]
                low_im, top_im = spec_ref[im_at, :TILE], spec_ref[im_at, TILE:]
                for p, part in zip(pair, parts):
                    low, top = low_ref[i, p:p + 1, :], top_ref[i, p:p + 1, :]
                    part.append(low * low_re - top * top_im)
                    part.append(low * low_im + top * top_re)
            return jnp.concatenate([jnp.concatenate(part, 0) for part in parts], 1).astype(bf16)

        def along_i(*pair):
            value = dot(matrix_ref[5], weighted(*pair)).astype(bf16)
            return [jnp.concatenate([value[:rows, TILE * t:TILE * (t + 1)], value[rows:, TILE * t:TILE * (t + 1)]], 1)
                    for t in range(len(pair))]

        for first in range(0, dirs, batch):
            stack = along_i(2 * dirs) if first == 0 else []
            for p in range(first, min(first + batch, dirs)):
                stack += along_i(p, dirs + p)
            value = dot(jnp.concatenate(stack, 0), matrix_ref[6])
            skip = rows if first == 0 else 0
            total = gain_ref[...] if first else -moved_ref[...].reshape(rows, PLANE) * value[:rows]
            for at in range(skip, value.shape[0], 2 * rows):
                total = total + value[at:at + rows] * value[at + rows:at + 2 * rows]
            gain_ref[...] = total
            next(beside, None)
        for _ in beside:
            pass
        now = moved_ref[...]
        collision = gain_ref[...].reshape(N, CELLS, PLANE)
        moved_ref[...] = jnp.where(cells_of(step)[1] == 0.0, now + collision_timestep * collision, now)
        for flip, out_ref in enumerate(outs):
            at = lax.bitwise_xor(rank, flip) * per
            for i in range(per):
                out_ref[step, :, PLANE * i:PLANE * (i + 1)] = moved_ref[at + i]

    opening = prepare(0, moved_refs[0], spec_refs[0])
    next(opening)
    copies[0].wait()
    for _ in opening:
        pass
    copies[1].wait()
    copies[2].wait()

    def two_rows(pair, _):
        finish(2 * pair, moved_refs[0], spec_refs[0], prepare(2 * pair + 1, moved_refs[1], spec_refs[1]))
        finish(2 * pair + 1, moved_refs[1], spec_refs[1], prepare(2 * pair + 2, moved_refs[0], spec_refs[0]))
        return 0

    lax.fori_loop(0, (steps - 1) // 2, two_rows, 0)
    if steps % 2 == 0:
        finish(steps - 2, moved_refs[0], spec_refs[0], prepare(steps - 1, moved_refs[1], spec_refs[1]))
    last = (steps - 1) % 2
    finish(steps - 1, moved_refs[last], spec_refs[last], iter(()))


def place_body(groups, places, rank_ref, *refs):
    pieces, refs = refs[:len(places)], refs[len(places):]
    out_ref, sems = refs[-2:]
    own_rows = out_ref.shape[0] // groups
    copies = []
    for at, (piece, (flip, first_row)) in enumerate(zip(pieces, places)):
        top = lax.bitwise_xor(rank_ref[0], flip) * own_rows + first_row
        copies.append(pltpu.make_async_copy(piece, out_ref.at[pl.ds(top, piece.shape[0])], sems.at[at]))
    for copy in copies:
        copy.start()
    for copy in copies:
        copy.wait()


def collide(rank, sources, carried, before, after, density, kinds, tables, low, top, matrices, earlier, first_row, steps):
    groups = len(sources)
    dirs = low.shape[1] // 3
    _, cols, width = sources[0].shape
    vmem = pl.BlockSpec(memory_space=pltpu.VMEM)
    shape = jax.ShapeDtypeStruct((steps, cols, width), f32)
    operands = (*sources, *carried, before, after, density, kinds, tables, low, top, matrices, earlier)
    cells = pltpu.VMEM((N, CELLS, PLANE), f32)
    spec = pltpu.VMEM((2 * N * CELLS, PLANE), f32)
    return call(
        functools.partial(collide_body, groups, dirs, 4, first_row, bool(carried)), (shape,) * groups, (rank, *operands),
        flops=steps * 2 * PLANE ** 3 * (2 * dirs + 6), limit=6,
        scratch=[cells, cells, spec, spec, pltpu.VMEM((N * CELLS, PLANE), f32)]
        + [pltpu.VMEM(value.shape, value.dtype) for value in (matrices, low, top)] + [pltpu.SemaphoreType.DMA((3,))],
        in_specs=[pl.BlockSpec(memory_space=pltpu.SMEM)] + [vmem] * (len(operands) - 1) + [pl.BlockSpec(memory_space=pl.ANY)],
        out_specs=(vmem,) * groups,
    )


def on_device(distribution, cell_type, first_kernel, second_kernel, loss_kernel):
    rows, cols, width = distribution.shape
    groups = lax.axis_size("vel")
    rank = lax.axis_index("vel")
    spots = lax.axis_size("cell")
    own_rows = rows // groups
    half = (own_rows // 4) * 2
    chunks = [(0, half), (half, own_rows - half)]
    rank_word = rank.astype(jnp.int32)[None]
    tables = jnp.asarray(velocity_tables())
    kinds = cell_type.astype(f32).T
    vmem = pl.BlockSpec(memory_space=pltpu.VMEM)
    smem = pl.BlockSpec(memory_space=pltpu.SMEM)
    anywhere = pl.BlockSpec(memory_space=pl.ANY)

    def swap(values):
        swapped = {0: values[0]}
        for flip in reversed(range(1, groups)):
            swapped[flip] = lax.ppermute(values[flip], "vel", [(i, i ^ flip) for i in range(groups)])
        return [swapped[flip] for flip in range(groups)]

    def cut(first_row, count, earlier, *columns):
        block = jax.ShapeDtypeStruct((count + 2, cols, width), f32)
        return call(
            functools.partial(cut_body, groups, first_row, count), (block,) * groups, (rank_word, distribution, earlier, *columns),
            in_specs=[smem, anywhere, anywhere] + [vmem] * len(columns), out_specs=(vmem,) * groups,
            scratch=[pltpu.SemaphoreType.DMA((groups,))])

    def rims(first_row, count, sources, carried=(), passing=()):
        edge = jax.ShapeDtypeStruct((count * N, 1, TILE), f32)
        same = [jax.ShapeDtypeStruct(value.shape, f32) for value in passing]
        keep = [] if carried else [jax.ShapeDtypeStruct((2, cols, width), f32)] * groups
        before = 1 + len(sources) + len(carried) + 3
        return call(
            functools.partial(edges_body, groups, first_row, count, len(passing), bool(carried)),
            (edge, edge, jax.ShapeDtypeStruct((cols, TILE), f32), *same, *keep),
            (rank_word, *sources, *carried, matrices, kinds, tables, *passing),
            in_specs=[smem] + [vmem] * (before - 4) + [anywhere, vmem, vmem] + [anywhere] * len(passing),
            out_specs=(vmem,) * 3 + (anywhere,) * len(passing) + (vmem,) * len(keep),
            input_output_aliases={before + at: 3 + at for at in range(len(passing))})

    def to_neighbours(first, last):
        return (lax.ppermute(last, "cell", [(i, i + 1) for i in range(spots - 1)]),
                lax.ppermute(first, "cell", [(i + 1, i) for i in range(spots - 1)]))

    (first_row, count), (next_row, next_count) = chunks
    cuts = [lax.dynamic_slice_in_dim(distribution, window(rank ^ flip, own_rows, rows, first_row, count), count + 2, 0)
            for flip in range(groups)]
    sources = swap(cuts)
    low, top, matrices = setup(first_kernel, second_kernel, loss_kernel)
    column = jax.ShapeDtypeStruct((rows, 1, width // 2 + TILE), f32)
    columns = to_neighbours(*call(
        columns_body, (column, column), (distribution, kinds, cuts[0]), in_specs=[vmem, vmem, anywhere], out_specs=(vmem,) * 2))
    first, last, density, *carried = rims(first_row, count, sources)
    edges = to_neighbours(first, last)
    following = cut(next_row, next_count, density, *columns)
    done = collide(rank_word, sources, (), *edges, density, kinds, tables, low, top, matrices, following[0], first_row, count)
    sources = swap(following)
    after, before, density, *done = rims(next_row, next_count, sources, carried, done)
    home = swap(done)
    done = collide(rank_word, sources, carried, before, after, density, kinds, tables, low, top, matrices, done[0], next_row, next_count)
    pieces = (*home, *swap(done))
    places = [(flip, row) for row in (first_row, next_row) for flip in range(groups)]
    return call(
        functools.partial(place_body, groups, places), jax.ShapeDtypeStruct(distribution.shape, f32),
        (rank_word, *pieces), in_specs=[smem] + [vmem] * len(pieces), out_specs=anywhere,
        scratch=[pltpu.SemaphoreType.DMA((len(pieces),))])


def solution(mesh):
    return jax.shard_map(
        on_device,
        mesh=mesh,
        in_specs=(P(None, "cell", "vel"), P(None, "cell"), P(), P(), P()),
        out_specs=P(None, "cell", "vel"),
        check_vma=False,
    )
```
